32 devices in a mesh: chan: 4 (over y, x), ctx: 8 (over z, core).
Axes of the slice: x: 2, y: 2, z: 4, core: 2. Of those that a mesh axis runs over, the one named last changes fastest.
Arguments:
- gate_stream: bfloat16 [2048, 4096], P('ctx', 'chan'), may hold values from -6 to 6
- key_stream: bfloat16 [2048, 4096], P('ctx', 'chan'), may hold values from -6 to 6
- value_stream: bfloat16 [2048, 4096], P('ctx', 'chan'), may hold values from -6 to 6
- residues: float32 [16, 4096], P(None, 'chan'), may hold values from -4 to 4
- decay_rates: float32 [16, 4096], P(None, 'chan'), may hold values from 9.765625e-06 to 0.05
- out_weight: bfloat16 [4096, 4096], P('chan'), may hold values from -0.125 to 0.125
Outputs:
- projected: bfloat16 [2048, 4096], P('ctx', 'chan')
The draws below stay inside these ranges and needn't reach their ends.
All inputs are finite; a program needn't handle non-finite values.
Results may differ from the reference program's by a relative error of at most 0.006.
Values sent between devices are 32-bit elements; how exact they have to be, the bound alone decides.
A program may use at most 64 MiB of HBM per device.

```python
import math
import jax
import jax.numpy as jnp
from jax import lax

CH = 4096
ORDER = 16
SEQ = 2048


def raised(result, rng, source, target, blocks, factor):
    owner, partner = [(jnp.arange(result.shape[position]) // (result.shape[position] // blocks)).reshape([-1 if axis == position else 1 for axis in range(result.ndim)]) for position in (source, target)]
    chosen = jax.random.permutation(rng, blocks)[partner]
    strong = (owner == chosen) | (owner == (partner + blocks // 2) % blocks)
    return jnp.where(strong, factor * result, result)


def block_levels(key, extent, split, smallest, largest):
    def one(dim, parts):
        draws = jax.random.uniform(jax.random.fold_in(jax.random.fold_in(key, 6), dim), (parts,), jnp.float32, smallest / len(split), largest / len(split))
        return jnp.repeat(jnp.exp(draws), extent[dim] // parts).reshape((-1,) + (1,) * (len(extent) - dim - 1))

    level = one(*split[0])
    for cut in split[1:]:
        level = level * one(*cut)
    return level


def bell_draw(stream_key, extent, spread, limit, pieces=(), kind=jnp.bfloat16):
    gain = block_levels(stream_key, extent, pieces, -0.22, 0.18) if pieces else 1.0
    values = jax.random.normal(stream_key, extent, jnp.float32) * spread * gain
    return jnp.minimum(jnp.maximum(values, -limit), limit).astype(kind)


def noise_with(rng, dims, deviation, bound, cuts, heavy, kind=jnp.bfloat16):
    entries = deviation * jax.random.normal(rng, dims, jnp.float32)
    if cuts:
        entries = entries * block_levels(rng, dims, cuts, -0.22, 0.18)
    return jnp.clip(raised(entries, jax.random.fold_in(rng, 3), *heavy), -bound, bound).astype(kind)


def setup_inputs(seed: int = 0) -> dict:
    splits = jax.random.split(jax.random.key(seed), 7)
    gate_stream = bell_draw(splits[0], (SEQ, CH), 1.0, 6.0, ((0, 8), (1, 4)))
    key_stream = bell_draw(splits[1], (SEQ, CH), 1.0, 6.0, ((0, 8), (1, 4)))
    value_stream = bell_draw(splits[2], (SEQ, CH), 1.0, 6.0, ((0, 8), (1, 4)))
    residues = bell_draw(splits[3], (ORDER, CH), 0.25, 4.0, ((1, 4),), jnp.float32)
    decay_rates = jnp.clip(jnp.exp(math.log(0.05) - 8.54091 * jax.random.uniform(splits[4], (ORDER, CH), jnp.float32) ** block_levels(splits[4], (ORDER, CH), ((1, 4),), -0.2, 0.2)), 9.765624781721272e-06, 0.05)
    out_weight = noise_with(splits[5], (CH, CH), CH ** -0.5, 0.125, ((0, 4),), (0, 1, 4, 2.0))
    return dict(gate_stream=gate_stream, key_stream=key_stream, value_stream=value_stream, residues=residues, decay_rates=decay_rates, out_weight=out_weight)


def convolve_block(operands):
    mixed_blk, resid_blk, decay_blk = operands
    steps_t = jnp.arange(SEQ, dtype=jnp.float32)[:, None, None]
    scale = resid_blk * jnp.sqrt(-jnp.expm1(-2.0 * decay_blk))
    filt = lax.optimization_barrier(jnp.sum(scale[None] * jnp.exp(-decay_blk[None] * steps_t), axis=1))
    total = 2 * SEQ
    mixed_f = jnp.fft.rfft(mixed_blk, n=total, axis=0)
    filt_f = jnp.fft.rfft(filt, n=total, axis=0)
    return jnp.fft.irfft(mixed_f * filt_f, n=total, axis=0)[:SEQ]

def reference(gate_stream, key_stream, value_stream, residues, decay_rates, out_weight):
    block = min(256, CH)
    count = CH // block
    mixed = key_stream.astype(jnp.float32) * value_stream.astype(jnp.float32)
    mixed_blocks = jnp.transpose(mixed.reshape(SEQ, count, block), (1, 0, 2))
    resid_blocks = jnp.transpose(residues.reshape(ORDER, count, block), (1, 0, 2))
    decay_blocks = jnp.transpose(decay_rates.reshape(ORDER, count, block), (1, 0, 2))
    conv = lax.map(convolve_block, (mixed_blocks, resid_blocks, decay_blocks))
    conv = jnp.transpose(conv, (1, 0, 2)).reshape(SEQ, CH)
    gated = (gate_stream.astype(jnp.float32) * conv).astype(jnp.bfloat16)
    return jnp.dot(gated, out_weight, preferred_element_type=jnp.float32).astype(jnp.bfloat16)
```

```python
import functools
import math

import jax
import jax.numpy as jnp
from jax import lax
from jax.experimental import pallas as pl
from jax.experimental.pallas import tpu as pltpu
from jax.sharding import PartitionSpec as P

HIGH = lax.Precision.HIGHEST
TWO_PI = 2.0 * math.pi


def swapped(block, axis, distance):
    count = lax.axis_size(axis)
    route = []
    for low in range(count):
        high = low | 1 << distance
        if high != low and high < count:
            route += [(low, high), (high, low)]
    return lax.ppermute(block, axis, route)


def unit_circle(numer, denom):
    angle = TWO_PI * numer.astype(jnp.float32) / denom
    return (jnp.cos(angle), jnp.sin(angle))


def times(ar, ai, br, bi):
    return (ar * br - ai * bi, ar * bi + ai * br)


def dft_matrix(length, inverse):
    index = jnp.arange(length, dtype=jnp.int32)
    cosine, sine = unit_circle(index[:, None] * index[None, :] % length, length)
    if inverse:
        top = jnp.concatenate([cosine, sine], axis=1)
        bottom = jnp.concatenate([-sine, cosine], axis=1)
    else:
        top = jnp.concatenate([cosine, -sine], axis=1)
        bottom = jnp.concatenate([sine, cosine], axis=1)
    return jnp.concatenate([top, bottom], axis=0)


def along_time(real_part, imag_part, matrix):
    rows = real_part.shape[-1]
    stacked = jnp.concatenate([real_part, imag_part], axis=-1)
    result = jnp.dot(stacked, matrix, precision=HIGH)
    return (result[..., :rows], result[..., rows:])


def filter_terms(residues, decay_rates, length):
    lam = jnp.exp(-decay_rates)
    one_less = -jnp.expm1(-decay_rates)
    base = residues * jnp.sqrt(-jnp.expm1(-2.0 * decay_rates))
    tail = jnp.exp(-decay_rates * length)
    return (base, lam, one_less, tail)


def response(freq, total, filt):
    base, lam, one_less, tail = filt
    wrapped = freq % total
    cosine, sine = unit_circle(wrapped, total)
    half_sine = jnp.sin(math.pi * wrapped.astype(jnp.float32) / total)
    parity_sign = 1.0 - 2.0 * (wrapped % 2).astype(jnp.float32)
    resp_r = 0.0
    resp_i = 0.0
    for mode in range(base.shape[0]):
        numer = base[mode] * (1.0 - tail[mode] * parity_sign)
        den_r = one_less[mode] + 2.0 * lam[mode] * half_sine * half_sine
        den_i = lam[mode] * sine
        norm_sq = den_r * den_r + den_i * den_i
        resp_r = resp_r + numer * den_r / norm_sq
        resp_i = resp_i - numer * den_i / norm_sq
    return (resp_r, resp_i)


def spectral(spec_r, spec_i, q_index, filt, big_p, rows):
    total = 2 * big_p * rows
    fsel = jnp.arange(2, dtype=jnp.int32).reshape((2,) + (1,) * (spec_r.ndim - 1))
    freq = 2 * q_index + fsel
    pos = jnp.arange(rows, dtype=jnp.int32)
    cosine, sine = unit_circle(pos * freq % total, total)
    tw_r, tw_i = times(spec_r, spec_i, cosine, -sine)
    full_r, full_i = along_time(tw_r, tw_i, dft_matrix(rows, False))
    resp_r, resp_i = response(freq + 2 * big_p * pos, total, filt)
    prod_r, prod_i = times(full_r, full_i, resp_r, resp_i)
    back_r, back_i = along_time(prod_r, prod_i, dft_matrix(rows, True))
    return times(back_r, back_i, cosine, sine)


def pre_twiddle(mixed, p_index, big_p, shape_f):
    fsel = jnp.arange(2, dtype=jnp.int32).reshape(shape_f)
    cosine, sine = unit_circle(p_index * fsel % (2 * big_p), 2 * big_p)
    return (mixed * cosine, -mixed * sine)


def post_twiddle(spec_r, spec_i, p_index, big_p, rows, shape_f):
    fsel = jnp.arange(2, dtype=jnp.int32).reshape(shape_f)
    cosine, sine = unit_circle(p_index * fsel % (2 * big_p), 2 * big_p)
    return jnp.sum(cosine * spec_r - sine * spec_i, axis=0) / (2.0 * big_p * rows)


def reverse_bits(device, bits):
    result = jnp.zeros_like(device)
    for bit in range(bits):
        result = result | (device >> bit & 1) << bits - 1 - bit
    return result


def butterfly_forward(real_part, imag_part, device, bits):
    for bit in range(bits - 1, -1, -1):
        half = 1 << bit
        place = device % (2 * half)
        upper = place >= half
        other_r, other_i = swapped((real_part, imag_part), "ctx", bit)
        cosine, sine = unit_circle(jnp.where(upper, place - half, 0), 2 * half)
        tw_r, tw_i = times(other_r - real_part, other_i - imag_part, cosine, -sine)
        real_part = jnp.where(upper, tw_r, real_part + other_r)
        imag_part = jnp.where(upper, tw_i, imag_part + other_i)
    return (real_part, imag_part)


def butterfly_inverse(real_part, imag_part, device, bits):
    for bit in range(bits):
        half = 1 << bit
        place = device % (2 * half)
        upper = place >= half
        cosine, sine = unit_circle(jnp.where(upper, place - half, 0), 2 * half)
        tw_r, tw_i = times(real_part, imag_part, cosine, sine)
        send_r = jnp.where(upper, tw_r, real_part)
        send_i = jnp.where(upper, tw_i, imag_part)
        other_r, other_i = swapped((send_r, send_i), "ctx", bit)
        real_part = jnp.where(upper, other_r - tw_r, real_part + other_r)
        imag_part = jnp.where(upper, other_i - tw_i, imag_part + other_i)
    return (real_part, imag_part)


def on_device(gate_stream, key_stream, value_stream, residues, decay_rates, out_weight):
    big_p = lax.axis_size("ctx")
    bits = big_p.bit_length() - 1
    rows = key_stream.shape[0]
    length = float(big_p * rows)
    device = lax.axis_index("ctx")
    mixed = jnp.transpose(key_stream.astype(jnp.float32) * value_stream.astype(jnp.float32))
    base, lam, one_less, tail = filter_terms(residues, decay_rates, length)
    filt = (base[:, :, None], lam[:, :, None], one_less[:, :, None], tail[:, :, None])
    z_r, z_i = pre_twiddle(mixed, device, big_p, (2, 1, 1))
    y_r, y_i = butterfly_forward(z_r, z_i, device, bits)
    q_index = reverse_bits(device, bits)
    u_r, u_i = spectral(y_r, y_i, q_index, filt, big_p, rows)
    v_r, v_i = butterfly_inverse(u_r, u_i, device, bits)
    conv_t = post_twiddle(v_r, v_i, device, big_p, rows, (2, 1, 1))
    conv_rows = jnp.transpose(conv_t)
    gated = (gate_stream.astype(jnp.float32) * conv_rows).astype(jnp.bfloat16)
    partial_terms = jnp.dot(gated, out_weight, preferred_element_type=jnp.float32)
    return lax.psum_scatter(partial_terms, "chan", scatter_dimension=1, tiled=True).astype(
        jnp.bfloat16
    )


MESH = pl.DeviceIdType.MESH
LANES = 128
SUB = 8
WIDE = 256
CHUNKS = 16
FORWARDS = 4


def tree_sum(terms):
    while len(terms) > 1:
        pairs = [terms[i] + terms[i + 1] for i in range(0, len(terms) - 1, 2)]
        terms = pairs + terms[len(pairs) * 2 :]
    return terms[0]


def one_minus_exp(u):
    series = u * (1.0 - u / 2.0 * (1.0 - u / 3.0 * (1.0 - u / 4.0 * (1.0 - u / 5.0 * (1.0 - u / 6.0)))))
    return jnp.where(u > 0.25, 1.0 - jnp.exp(-u), series)


def kernel(
    stages,
    gate_hbm, key_hbm, value_hbm, res_hbm, decay_hbm, w_hbm, out_hbm,
    gate, key, value, res, decay, wbuf, sbuf, rbuf, obuf, gated,
    xs, ys, lam, base, dec, ends, give, chip, peer_end, zbuf, give_state, peer_state, state,
    in_sem, w_sem, out_sem, chunk_send, chunk_recv, pair_send, pair_recv, z_send, z_recv,
):
    rows = gate.shape[0]
    modes = res.shape[0]
    half_modes = modes // 2
    half_size = half_modes * SUB
    chan = lax.axis_index("chan")
    ctx = lax.axis_index("ctx")
    core = lax.rem(ctx, 2)
    stage = ctx // 2
    x = lax.rem(chan, 2)
    y = chan // 2
    along_x = y * 2 + (1 - x)
    along_y = (1 - y) * 2 + x
    across = (1 - y) * 2 + (1 - x)
    partner = stage * 2 + (1 - core)

    loads = [
        pltpu.make_async_copy(src, dst, in_sem.at[i])
        for i, (src, dst) in enumerate(
            [(key_hbm, key), (value_hbm, value), (decay_hbm, decay), (res_hbm, res), (gate_hbm, gate)]
        )
    ]
    for load in loads:
        load.start()

    def w_copy(i):
        owner = (across, along_y if i % 2 else along_x, along_x if i % 2 else along_y, chan)[i // 4]
        column = owner * (4 * WIDE) + (i % 2) * 2 * WIDE + (i // 2 % 2) * WIDE
        return pltpu.make_async_copy(
            w_hbm.at[:, pl.ds(pl.multiple_of(column, WIDE), WIDE)], wbuf.at[i], w_sem.at[i]
        )

    for i in range(CHUNKS):
        w_copy(i).start()

    barrier = pltpu.get_barrier_semaphore()
    pl.semaphore_signal(barrier, inc=1, device_id=(along_x, ctx), device_id_type=MESH)
    pl.semaphore_signal(barrier, inc=1, device_id=(along_y, ctx), device_id_type=MESH)
    pl.semaphore_signal(barrier, inc=1, device_id=(chan, partner), device_id_type=MESH)
    for step in range(1, stages):
        other = lax.rem(stage + step, stages) * 2 + core
        pl.semaphore_signal(barrier, inc=1, device_id=(chan, other), device_id_type=MESH)

    loads[2].wait()
    loads[3].wait()
    for b in range(SUB):
        at = pl.ds(b, modes, stride=SUB)
        d = decay[:, b * LANES : (b + 1) * LANES]
        dec[at, :] = d
        lam[at, :] = jnp.exp(-d)
        base[at, :] = res[:, b * LANES : (b + 1) * LANES] * jnp.sqrt(one_minus_exp(2.0 * d))
    loads[0].wait()
    loads[1].wait()
    for b in range(SUB):
        cols = slice(b * LANES, (b + 1) * LANES)
        xs[pl.ds(b, rows, stride=SUB), :] = key[:, cols].astype(jnp.float32) * value[:, cols].astype(jnp.float32)

    def vec(t):
        return pl.ds(pl.multiple_of(t * SUB, SUB), SUB)

    def mode_rows(half, n):
        return pl.ds(pl.multiple_of(half * half_size + n * SUB, SUB), SUB)

    def half_rows(half):
        return pl.ds(pl.multiple_of(half * half_size, half_size), half_size)

    mid = rows // 2

    def end_states(half, dst):
        lams = [lam[mode_rows(half, n), :] for n in range(half_modes)]

        def step(t, carry):
            low, high = carry
            x_low = xs[vec(t), :]
            x_high = xs[vec(t + mid), :]
            low = tuple(l * h + x_low for l, h in zip(lams, low))
            high = tuple(l * h + x_high for l, h in zip(lams, high))
            return (low, high)

        zero = tuple(jnp.zeros((SUB, LANES), jnp.float32) for _ in range(half_modes))
        low, high = lax.fori_loop(0, mid, step, (zero, zero), unroll=4)
        for n in range(half_modes):
            shrink = jnp.exp(dec[mode_rows(half, n), :] * float(-mid))
            dst[n * SUB : (n + 1) * SUB, :] = shrink * low[n] + high[n]

    end_states(1 - core, give)
    pl.semaphore_wait(barrier, 3 + stages - 1)
    send_end = pltpu.make_async_remote_copy(
        src_ref=give, dst_ref=peer_end, send_sem=pair_send.at[0], recv_sem=pair_recv.at[0],
        device_id=(chan, partner), device_id_type=MESH,
    )
    send_end.start()
    end_states(core, ends)
    send_end.wait_recv()

    own_decay = dec[half_rows(core), :]
    span = jnp.exp(own_decay * float(-rows))
    is_first = core == 0
    end_first = jnp.where(is_first, ends[...], peer_end[...])
    end_second = jnp.where(is_first, peer_end[...], ends[...])
    chip[...] = span * end_first + end_second

    def push(step):
        return pltpu.make_async_remote_copy(
            src_ref=chip, dst_ref=zbuf.at[step - 1], send_sem=z_send.at[step - 1], recv_sem=z_recv.at[step - 1],
            device_id=(chan, lax.rem(stage + step, stages) * 2 + core), device_id_type=MESH,
        )

    for step in range(1, stages):
        @pl.when(stage + step < stages)
        def _():
            push(step).start()

    lams = [lam[n * SUB : (n + 1) * SUB, :] for n in range(modes)]
    bases = [base[n * SUB : (n + 1) * SUB, :] for n in range(modes)]

    def local_step(t, hidden):
        now = xs[vec(t), :]
        hidden = tuple(l * h + now for l, h in zip(lams, hidden))
        ys[vec(t), :] = tree_sum([b * h for b, h in zip(bases, hidden)])
        return hidden

    zero = tuple(jnp.zeros((SUB, LANES), jnp.float32) for _ in range(modes))
    lax.fori_loop(0, rows, local_step, zero, unroll=4)

    state[...] = jnp.zeros_like(state)
    for step in range(1, stages):
        @pl.when(stage >= step)
        def _():
            push(step).wait_recv()
            weight = jnp.exp(dec[half_rows(core), :] * float(-2 * rows * (step - 1)))
            state[...] += weight * zbuf[step - 1]

    begin_first = state[...]
    begin_second = span * begin_first + end_first
    give_state[...] = jnp.where(is_first, begin_second, begin_first)
    send_state = pltpu.make_async_remote_copy(
        src_ref=give_state, dst_ref=peer_state, send_sem=pair_send.at[1], recv_sem=pair_recv.at[1],
        device_id=(chan, partner), device_id_type=MESH,
    )
    send_state.start()
    state[...] = jnp.where(is_first, begin_first, begin_second)

    def add_state(half, src):
        lams = [lam[mode_rows(half, n), :] for n in range(half_modes)]
        low = tuple(base[mode_rows(half, n), :] * src[n * SUB : (n + 1) * SUB, :] for n in range(half_modes))
        high = tuple(jnp.exp(dec[mode_rows(half, n), :] * float(-mid)) * low[n] for n in range(half_modes))

        def step(t, carry):
            low, high = carry
            low = tuple(l * h for l, h in zip(lams, low))
            high = tuple(l * h for l, h in zip(lams, high))
            ys[vec(t), :] += tree_sum(list(low))
            ys[vec(t + mid), :] += tree_sum(list(high))
            return (low, high)

        lax.fori_loop(0, mid, step, (low, high), unroll=4)

    add_state(core, state)
    send_state.wait_recv()
    add_state(1 - core, peer_state)

    loads[4].wait()
    for b in range(SUB):
        cols = slice(b * LANES, (b + 1) * LANES)
        conv = ys[pl.ds(b, rows, stride=SUB), :]
        gated[:, cols] = (gate[:, cols].astype(jnp.float32) * conv).astype(jnp.bfloat16)

    def chunk_copy(i, target):
        return pltpu.make_async_remote_copy(
            src_ref=sbuf.at[i], dst_ref=rbuf.at[i], send_sem=chunk_send.at[i], recv_sem=chunk_recv.at[i],
            device_id=(target, ctx), device_id_type=MESH,
        )

    def first_target(i):
        odd = lax.rem(i, 2)
        return along_x * (1 - odd) + along_y * odd

    def second_target(i):
        odd = lax.rem(i, 2)
        return along_y * (1 - odd) + along_x * odd

    @pl.loop(0, CHUNKS)
    def _(i):
        pltpu.make_async_copy(w_hbm.at[:, pl.ds(0, WIDE)], wbuf.at[i], w_sem.at[i]).wait()
        sbuf[i] = jnp.dot(gated[...], wbuf[i], preferred_element_type=jnp.float32)

        @pl.when(i < 2 * FORWARDS)
        def _():
            chunk_copy(i, first_target(i)).start()

    @pl.loop(0, FORWARDS)
    def _(j):
        chunk_copy(j, first_target(j)).wait_recv()
        sbuf[j + 2 * FORWARDS] += rbuf[j]
        chunk_copy(j + 2 * FORWARDS, second_target(j)).start()

    def out_copy(j):
        column = lax.rem(j, 2) * (2 * WIDE) + (j // 2) * WIDE
        return pltpu.make_async_copy(
            obuf.at[j], out_hbm.at[:, pl.ds(pl.multiple_of(column, WIDE), WIDE)], out_sem.at[j]
        )

    @pl.loop(0, FORWARDS)
    def _(j):
        chunk_copy(j + FORWARDS, first_target(j)).wait_recv()
        sbuf[j + 3 * FORWARDS] += rbuf[j + FORWARDS]

    @pl.loop(0, FORWARDS)
    def _(j):
        chunk_copy(j + 2 * FORWARDS, second_target(j)).wait_recv()
        obuf[j] = (sbuf[j + 3 * FORWARDS] + rbuf[j + 2 * FORWARDS]).astype(jnp.bfloat16)
        out_copy(j).start()

    send_end.wait_send()
    send_state.wait_send()
    for step in range(1, stages):
        @pl.when(stage + step < stages)
        def _():
            push(step).wait_send()

    @pl.loop(0, 2 * FORWARDS)
    def _(i):
        chunk_copy(i, first_target(i)).wait_send()

    @pl.loop(0, FORWARDS)
    def _(j):
        chunk_copy(j + 2 * FORWARDS, second_target(j)).wait_send()
        out_copy(j).wait()


def fused(gate_stream, key_stream, value_stream, residues, decay_rates, out_weight):
    rows, channels = gate_stream.shape
    modes = residues.shape[0]
    stages = lax.axis_size("ctx") // 2
    f32, bf16 = jnp.float32, jnp.bfloat16
    whole = (modes * SUB, LANES)
    half = (modes // 2 * SUB, LANES)
    dma = pltpu.SemaphoreType.DMA
    return pl.pallas_call(
        functools.partial(kernel, stages),
        out_shape=jax.ShapeDtypeStruct((rows, 4 * WIDE), bf16),
        in_specs=[pl.BlockSpec(memory_space=pl.ANY)] * 6,
        out_specs=pl.BlockSpec(memory_space=pl.ANY),
        scratch_shapes=[
            pltpu.VMEM((rows, channels), bf16),
            pltpu.VMEM((rows, channels), bf16),
            pltpu.VMEM((rows, channels), bf16),
            pltpu.VMEM((modes, channels), f32),
            pltpu.VMEM((modes, channels), f32),
            pltpu.VMEM((CHUNKS, channels, WIDE), bf16),
            pltpu.VMEM((CHUNKS, rows, WIDE), f32),
            pltpu.VMEM((3 * FORWARDS, rows, WIDE), f32),
            pltpu.VMEM((FORWARDS, rows, WIDE), bf16),
            pltpu.VMEM((rows, channels), bf16),
            pltpu.VMEM((rows * SUB, LANES), f32),
            pltpu.VMEM((rows * SUB, LANES), f32),
            pltpu.VMEM(whole, f32),
            pltpu.VMEM(whole, f32),
            pltpu.VMEM(whole, f32),
            pltpu.VMEM(half, f32),
            pltpu.VMEM(half, f32),
            pltpu.VMEM(half, f32),
            pltpu.VMEM(half, f32),
            pltpu.VMEM((stages - 1,) + half, f32),
            pltpu.VMEM(half, f32),
            pltpu.VMEM(half, f32),
            pltpu.VMEM(half, f32),
            dma((5,)),
            dma((CHUNKS,)),
            dma((FORWARDS,)),
            dma((3 * FORWARDS,)),
            dma((3 * FORWARDS,)),
            dma((2,)),
            dma((2,)),
            dma((stages - 1,)),
            dma((stages - 1,)),
        ],
        compiler_params=pltpu.CompilerParams(
            collective_id=0, has_side_effects=True, vmem_limit_bytes=48 * 1024 * 1024
        ),
        cost_estimate=pl.CostEstimate(
            flops=2 * rows * channels * 16 * WIDE, bytes_accessed=2 * channels * 16 * WIDE, transcendentals=0
        ),
    )(gate_stream, key_stream, value_stream, residues, decay_rates, out_weight)


def run(*arrays):
    square = lax.axis_size("chan") == 4 and lax.axis_size("ctx") % 2 == 0 and lax.axis_size("ctx") > 2
    fits = arrays[0].shape[1] == SUB * LANES and arrays[5].shape[1] == 16 * WIDE
    return (fused if square and fits else on_device)(*arrays)


def solution(mesh):
    return jax.shard_map(
        run,
        mesh=mesh,
        in_specs=(
            P("ctx", "chan"),
            P("ctx", "chan"),
            P("ctx", "chan"),
            P(None, "chan"),
            P(None, "chan"),
            P("chan", None),
        ),
        out_specs=P("ctx", "chan"),
        check_vma=False,
    )
```

```python
import functools
import math

import jax
import jax.numpy as jnp
from jax import lax
from jax.experimental import pallas as pl
from jax.experimental.pallas import tpu as pltpu
from jax.sharding import PartitionSpec as P

HIGH = lax.Precision.HIGHEST
TWO_PI = 2.0 * math.pi


def swapped(block, axis, distance):
    count = lax.axis_size(axis)
    route = []
    for low in range(count):
        high = low | 1 << distance
        if high != low and high < count:
            route += [(low, high), (high, low)]
    return lax.ppermute(block, axis, route)


def unit_circle(numer, denom):
    angle = TWO_PI * numer.astype(jnp.float32) / denom
    return (jnp.cos(angle), jnp.sin(angle))


def times(ar, ai, br, bi):
    return (ar * br - ai * bi, ar * bi + ai * br)


def dft_matrix(length, inverse):
    index = jnp.arange(length, dtype=jnp.int32)
    cosine, sine = unit_circle(index[:, None] * index[None, :] % length, length)
    if inverse:
        top = jnp.concatenate([cosine, sine], axis=1)
        bottom = jnp.concatenate([-sine, cosine], axis=1)
    else:
        top = jnp.concatenate([cosine, -sine], axis=1)
        bottom = jnp.concatenate([sine, cosine], axis=1)
    return jnp.concatenate([top, bottom], axis=0)


def along_time(real_part, imag_part, matrix):
    rows = real_part.shape[-1]
    stacked = jnp.concatenate([real_part, imag_part], axis=-1)
    result = jnp.dot(stacked, matrix, precision=HIGH)
    return (result[..., :rows], result[..., rows:])


def filter_terms(residues, decay_rates, length):
    lam = jnp.exp(-decay_rates)
    one_less = -jnp.expm1(-decay_rates)
    base = residues * jnp.sqrt(-jnp.expm1(-2.0 * decay_rates))
    tail = jnp.exp(-decay_rates * length)
    return (base, lam, one_less, tail)


def response(freq, total, filt):
    base, lam, one_less, tail = filt
    wrapped = freq % total
    cosine, sine = unit_circle(wrapped, total)
    half_sine = jnp.sin(math.pi * wrapped.astype(jnp.float32) / total)
    parity_sign = 1.0 - 2.0 * (wrapped % 2).astype(jnp.float32)
    resp_r = 0.0
    resp_i = 0.0
    for mode in range(base.shape[0]):
        numer = base[mode] * (1.0 - tail[mode] * parity_sign)
        den_r = one_less[mode] + 2.0 * lam[mode] * half_sine * half_sine
        den_i = lam[mode] * sine
        norm_sq = den_r * den_r + den_i * den_i
        resp_r = resp_r + numer * den_r / norm_sq
        resp_i = resp_i - numer * den_i / norm_sq
    return (resp_r, resp_i)


def spectral(spec_r, spec_i, q_index, filt, big_p, rows):
    total = 2 * big_p * rows
    fsel = jnp.arange(2, dtype=jnp.int32).reshape((2,) + (1,) * (spec_r.ndim - 1))
    freq = 2 * q_index + fsel
    pos = jnp.arange(rows, dtype=jnp.int32)
    cosine, sine = unit_circle(pos * freq % total, total)
    tw_r, tw_i = times(spec_r, spec_i, cosine, -sine)
    full_r, full_i = along_time(tw_r, tw_i, dft_matrix(rows, False))
    resp_r, resp_i = response(freq + 2 * big_p * pos, total, filt)
    prod_r, prod_i = times(full_r, full_i, resp_r, resp_i)
    back_r, back_i = along_time(prod_r, prod_i, dft_matrix(rows, True))
    return times(back_r, back_i, cosine, sine)


def pre_twiddle(mixed, p_index, big_p, shape_f):
    fsel = jnp.arange(2, dtype=jnp.int32).reshape(shape_f)
    cosine, sine = unit_circle(p_index * fsel % (2 * big_p), 2 * big_p)
    return (mixed * cosine, -mixed * sine)


def post_twiddle(spec_r, spec_i, p_index, big_p, rows, shape_f):
    fsel = jnp.arange(2, dtype=jnp.int32).reshape(shape_f)
    cosine, sine = unit_circle(p_index * fsel % (2 * big_p), 2 * big_p)
    return jnp.sum(cosine * spec_r - sine * spec_i, axis=0) / (2.0 * big_p * rows)


def reverse_bits(device, bits):
    result = jnp.zeros_like(device)
    for bit in range(bits):
        result = result | (device >> bit & 1) << bits - 1 - bit
    return result


def butterfly_forward(real_part, imag_part, device, bits):
    for bit in range(bits - 1, -1, -1):
        half = 1 << bit
        place = device % (2 * half)
        upper = place >= half
        other_r, other_i = swapped((real_part, imag_part), "ctx", bit)
        cosine, sine = unit_circle(jnp.where(upper, place - half, 0), 2 * half)
        tw_r, tw_i = times(other_r - real_part, other_i - imag_part, cosine, -sine)
        real_part = jnp.where(upper, tw_r, real_part + other_r)
        imag_part = jnp.where(upper, tw_i, imag_part + other_i)
    return (real_part, imag_part)


def butterfly_inverse(real_part, imag_part, device, bits):
    for bit in range(bits):
        half = 1 << bit
        place = device % (2 * half)
        upper = place >= half
        cosine, sine = unit_circle(jnp.where(upper, place - half, 0), 2 * half)
        tw_r, tw_i = times(real_part, imag_part, cosine, sine)
        send_r = jnp.where(upper, tw_r, real_part)
        send_i = jnp.where(upper, tw_i, imag_part)
        other_r, other_i = swapped((send_r, send_i), "ctx", bit)
        real_part = jnp.where(upper, other_r - tw_r, real_part + other_r)
        imag_part = jnp.where(upper, other_i - tw_i, imag_part + other_i)
    return (real_part, imag_part)


def on_device(gate_stream, key_stream, value_stream, residues, decay_rates, out_weight):
    big_p = lax.axis_size("ctx")
    bits = big_p.bit_length() - 1
    rows = key_stream.shape[0]
    length = float(big_p * rows)
    device = lax.axis_index("ctx")
    mixed = jnp.transpose(key_stream.astype(jnp.float32) * value_stream.astype(jnp.float32))
    base, lam, one_less, tail = filter_terms(residues, decay_rates, length)
    filt = (base[:, :, None], lam[:, :, None], one_less[:, :, None], tail[:, :, None])
    z_r, z_i = pre_twiddle(mixed, device, big_p, (2, 1, 1))
    y_r, y_i = butterfly_forward(z_r, z_i, device, bits)
    q_index = reverse_bits(device, bits)
    u_r, u_i = spectral(y_r, y_i, q_index, filt, big_p, rows)
    v_r, v_i = butterfly_inverse(u_r, u_i, device, bits)
    conv_t = post_twiddle(v_r, v_i, device, big_p, rows, (2, 1, 1))
    conv_rows = jnp.transpose(conv_t)
    gated = (gate_stream.astype(jnp.float32) * conv_rows).astype(jnp.bfloat16)
    partial_terms = jnp.dot(gated, out_weight, preferred_element_type=jnp.float32)
    return lax.psum_scatter(partial_terms, "chan", scatter_dimension=1, tiled=True).astype(
        jnp.bfloat16
    )


MESH = pl.DeviceIdType.MESH
LANES = 128
SUB = 8
WIDE = 512
CHUNKS = 16
FORWARDS = 4
SLABS = 4


def tree_sum(terms):
    while len(terms) > 1:
        pairs = [terms[i] + terms[i + 1] for i in range(0, len(terms) - 1, 2)]
        terms = pairs + terms[len(pairs) * 2 :]
    return terms[0]


def one_minus_exp(u):
    series = u * (1.0 - u / 2.0 * (1.0 - u / 3.0 * (1.0 - u / 4.0 * (1.0 - u / 5.0 * (1.0 - u / 6.0)))))
    return jnp.where(u > 0.25, 1.0 - jnp.exp(-u), series)


def kernel(
    stages,
    gate_hbm, key_hbm, value_hbm, res_hbm, decay_hbm, w_hbm, out_hbm,
    gate, key, value, res, decay, wbuf, sbuf, rbuf, obuf, gated,
    xs, ys, lam, base, dec, ends, give, chip, peer_end, zbuf, give_state, peer_state, state,
    in_sem, w_sem, out_sem, chunk_send, chunk_recv, pair_send, pair_recv, z_send, z_recv,
):
    rows = gate.shape[0]
    modes = res.shape[0]
    half_modes = modes // 2
    half_size = half_modes * SUB
    chan = lax.axis_index("chan")
    ctx = lax.axis_index("ctx")
    core = lax.rem(ctx, 2)
    stage = ctx // 2
    x = lax.rem(chan, 2)
    y = chan // 2
    along_x = y * 2 + (1 - x)
    along_y = (1 - y) * 2 + x
    across = (1 - y) * 2 + (1 - x)
    partner = stage * 2 + (1 - core)

    loads = [
        pltpu.make_async_copy(src, dst, in_sem.at[i])
        for i, (src, dst) in enumerate(
            [(decay_hbm, decay), (res_hbm, res), (gate_hbm, gate)]
        )
    ]
    slab = rows // SLABS

    def stream_load(i):
        src, dst = (key_hbm, key) if i % 2 == 0 else (value_hbm, value)
        here = pl.ds(i // 2 * slab, slab)
        return pltpu.make_async_copy(src.at[here, :], dst.at[here, :], in_sem.at[3 + i])

    for i in range(2 * SLABS):
        stream_load(i).start()
    for load in loads[:2]:
        load.start()

    def w_copy(i):
        owner = (across, along_y if i % 2 else along_x, along_x if i % 2 else along_y, chan)[i // 2]
        column = owner * (2 * WIDE) + (i % 2) * WIDE
        return pltpu.make_async_copy(
            w_hbm.at[:, pl.ds(pl.multiple_of(column, WIDE), WIDE)], wbuf.at[i], w_sem.at[i]
        )

    barrier = pltpu.get_barrier_semaphore()
    pl.semaphore_signal(barrier, inc=1, device_id=(along_x, ctx), device_id_type=MESH)
    pl.semaphore_signal(barrier, inc=1, device_id=(along_y, ctx), device_id_type=MESH)
    pl.semaphore_signal(barrier, inc=1, device_id=(chan, partner), device_id_type=MESH)
    for step in range(1, stages):
        other = lax.rem(stage + step, stages) * 2 + core
        pl.semaphore_signal(barrier, inc=1, device_id=(chan, other), device_id_type=MESH)

    loads[0].wait()
    loads[1].wait()
    for b in range(SUB):
        at = pl.ds(b, modes, stride=SUB)
        d = decay[:, b * LANES : (b + 1) * LANES]
        dec[at, :] = d
        lam[at, :] = jnp.exp(-d)
        base[at, :] = res[:, b * LANES : (b + 1) * LANES] * jnp.sqrt(one_minus_exp(2.0 * d))
    for part in range(SLABS):
        stream_load(2 * part).wait()
        stream_load(2 * part + 1).wait()
        here = slice(part * slab, (part + 1) * slab)
        for b in range(SUB):
            cols = slice(b * LANES, (b + 1) * LANES)
            mixed = key[here, cols].astype(jnp.float32) * value[here, cols].astype(jnp.float32)
            xs[pl.ds(part * slab * SUB + b, slab, stride=SUB), :] = mixed
    loads[2].start()
    for i in range(CHUNKS // 2):
        w_copy(i).start()

    def vec(t):
        return pl.ds(pl.multiple_of(t * SUB, SUB), SUB)

    def mode_rows(half, n):
        return pl.ds(pl.multiple_of(half * half_size + n * SUB, SUB), SUB)

    def half_rows(half):
        return pl.ds(pl.multiple_of(half * half_size, half_size), half_size)

    mid = rows // 2

    def end_states(half, dst):
        lams = [lam[mode_rows(half, n), :] for n in range(half_modes)]

        def step(t, carry):
            low, high = carry
            x_low = xs[vec(t), :]
            x_high = xs[vec(t + mid), :]
            low = tuple(l * h + x_low for l, h in zip(lams, low))
            high = tuple(l * h + x_high for l, h in zip(lams, high))
            return (low, high)

        zero = tuple(jnp.zeros((SUB, LANES), jnp.float32) for _ in range(half_modes))
        low, high = lax.fori_loop(0, mid, step, (zero, zero), unroll=4)
        for n in range(half_modes):
            shrink = jnp.exp(dec[mode_rows(half, n), :] * float(-mid))
            dst[n * SUB : (n + 1) * SUB, :] = shrink * low[n] + high[n]

    end_states(1 - core, give)
    pl.semaphore_wait(barrier, 3 + stages - 1)
    send_end = pltpu.make_async_remote_copy(
        src_ref=give, dst_ref=peer_end, send_sem=pair_send.at[0], recv_sem=pair_recv.at[0],
        device_id=(chan, partner), device_id_type=MESH,
    )
    send_end.start()
    end_states(core, ends)
    send_end.wait_recv()

    own_decay = dec[half_rows(core), :]
    span = jnp.exp(own_decay * float(-rows))
    is_first = core == 0
    end_first = jnp.where(is_first, ends[...], peer_end[...])
    end_second = jnp.where(is_first, peer_end[...], ends[...])
    chip[...] = span * end_first + end_second

    def push(step):
        return pltpu.make_async_remote_copy(
            src_ref=chip, dst_ref=zbuf.at[step - 1], send_sem=z_send.at[step - 1], recv_sem=z_recv.at[step - 1],
            device_id=(chan, lax.rem(stage + step, stages) * 2 + core), device_id_type=MESH,
        )

    for step in range(1, stages):
        @pl.when(stage + step < stages)
        def _():
            push(step).start()

    lams = [lam[n * SUB : (n + 1) * SUB, :] for n in range(modes)]
    bases = [base[n * SUB : (n + 1) * SUB, :] for n in range(modes)]

    def local_step(t, hidden):
        now = xs[vec(t), :]
        hidden = tuple(l * h + now for l, h in zip(lams, hidden))
        ys[vec(t), :] = tree_sum([b * h for b, h in zip(bases, hidden)])
        return hidden

    zero = tuple(jnp.zeros((SUB, LANES), jnp.float32) for _ in range(modes))
    lax.fori_loop(0, rows, local_step, zero, unroll=4)

    state[...] = jnp.zeros_like(state)
    for step in range(1, stages):
        @pl.when(stage >= step)
        def _():
            push(step).wait_recv()
            weight = jnp.exp(dec[half_rows(core), :] * float(-2 * rows * (step - 1)))
            state[...] += weight * zbuf[step - 1]

    begin_first = state[...]
    begin_second = span * begin_first + end_first
    give_state[...] = jnp.where(is_first, begin_second, begin_first)
    send_state = pltpu.make_async_remote_copy(
        src_ref=give_state, dst_ref=peer_state, send_sem=pair_send.at[1], recv_sem=pair_recv.at[1],
        device_id=(chan, partner), device_id_type=MESH,
    )
    send_state.start()
    state[...] = jnp.where(is_first, begin_first, begin_second)

    quarter = rows // 4

    def add_state(half, src, part):
        lams = [lam[mode_rows(half, n), :] for n in range(half_modes)]
        start = part * mid
        low, high = [], []
        for n in range(half_modes):
            d = dec[mode_rows(half, n), :]
            first = base[mode_rows(half, n), :] * src[n * SUB : (n + 1) * SUB, :]
            low.append(first * jnp.exp(d * float(-start)) if part else first)
            high.append(first * jnp.exp(d * float(-start - quarter)))

        def step(t, carry):
            low, high = carry
            low = tuple(l * h for l, h in zip(lams, low))
            high = tuple(l * h for l, h in zip(lams, high))
            ys[vec(t + start), :] += tree_sum(list(low))
            ys[vec(t + start + quarter), :] += tree_sum(list(high))
            return (low, high)

        lax.fori_loop(0, quarter, step, (tuple(low), tuple(high)), unroll=4)

    def gate_rows(part):
        here = slice(part * mid, (part + 1) * mid)
        for b in range(SUB):
            cols = slice(b * LANES, (b + 1) * LANES)
            conv = ys[pl.ds(part * mid * SUB + b, mid, stride=SUB), :]
            gated[here, cols] = (gate[here, cols].astype(jnp.float32) * conv).astype(jnp.bfloat16)

    def chunk_copy(i, target):
        return pltpu.make_async_remote_copy(
            src_ref=sbuf.at[i], dst_ref=rbuf.at[i], send_sem=chunk_send.at[i], recv_sem=chunk_recv.at[i],
            device_id=(target, ctx), device_id_type=MESH,
        )

    def first_target(i):
        odd = lax.rem(i, 2)
        return along_x * (1 - odd) + along_y * odd

    def second_target(i):
        odd = lax.rem(i, 2)
        return along_y * (1 - odd) + along_x * odd

    def w_wait(i):
        pltpu.make_async_copy(w_hbm.at[:, pl.ds(0, WIDE)], wbuf.at[i], w_sem.at[i]).wait()

    def block_of(i):
        return i // 4 * 2 + lax.rem(i, 2)

    def partial_sum(i):
        part = lax.rem(i // 2, 2)
        here = pl.ds(pl.multiple_of(part * mid, mid), mid)
        sbuf[i] = jnp.dot(gated[here, :], wbuf[block_of(i)], preferred_element_type=jnp.float32)

    add_state(core, state, 0)
    send_state.wait_recv()
    add_state(1 - core, peer_state, 0)
    loads[2].wait()
    gate_rows(0)

    @pl.loop(0, 2)
    def _(i):
        w_wait(i)
        partial_sum(i)
        chunk_copy(i, first_target(i)).start()

    add_state(core, state, 1)
    add_state(1 - core, peer_state, 1)
    gate_rows(1)

    @pl.loop(2, CHUNKS)
    def _(i):
        @pl.when(lax.rem(i // 2, 2) == 0)
        def _():
            w_wait(block_of(i))

        partial_sum(i)

        @pl.when(i < 2 * FORWARDS)
        def _():
            chunk_copy(i, first_target(i)).start()

    @pl.loop(0, FORWARDS)
    def _(j):
        chunk_copy(j, first_target(j)).wait_recv()
        sbuf[j + 2 * FORWARDS] += rbuf[j]
        chunk_copy(j + 2 * FORWARDS, second_target(j)).start()

    def out_copy(j):
        here = pl.ds(pl.multiple_of(j // 2 * mid, mid), mid)
        cols = pl.ds(pl.multiple_of(lax.rem(j, 2) * WIDE, WIDE), WIDE)
        return pltpu.make_async_copy(obuf.at[j], out_hbm.at[here, cols], out_sem.at[j])

    @pl.loop(0, FORWARDS)
    def _(j):
        chunk_copy(j + FORWARDS, first_target(j)).wait_recv()
        sbuf[j + 3 * FORWARDS] += rbuf[j + FORWARDS]

    @pl.loop(0, FORWARDS)
    def _(j):
        chunk_copy(j + 2 * FORWARDS, second_target(j)).wait_recv()
        obuf[j] = (sbuf[j + 3 * FORWARDS] + rbuf[j + 2 * FORWARDS]).astype(jnp.bfloat16)
        out_copy(j).start()

    send_end.wait_send()
    send_state.wait_send()
    for step in range(1, stages):
        @pl.when(stage + step < stages)
        def _():
            push(step).wait_send()

    @pl.loop(0, 2 * FORWARDS)
    def _(i):
        chunk_copy(i, first_target(i)).wait_send()

    @pl.loop(0, FORWARDS)
    def _(j):
        chunk_copy(j + 2 * FORWARDS, second_target(j)).wait_send()
        out_copy(j).wait()


def fused(gate_stream, key_stream, value_stream, residues, decay_rates, out_weight):
    rows, channels = gate_stream.shape
    modes = residues.shape[0]
    stages = lax.axis_size("ctx") // 2
    f32, bf16 = jnp.float32, jnp.bfloat16
    whole = (modes * SUB, LANES)
    half = (modes // 2 * SUB, LANES)
    dma = pltpu.SemaphoreType.DMA
    return pl.pallas_call(
        functools.partial(kernel, stages),
        out_shape=jax.ShapeDtypeStruct((rows, 2 * WIDE), bf16),
        in_specs=[pl.BlockSpec(memory_space=pltpu.HBM)] * 6,
        out_specs=pl.BlockSpec(memory_space=pltpu.HBM),
        scratch_shapes=[
            pltpu.VMEM((rows, channels), bf16),
            pltpu.VMEM((rows, channels), bf16),
            pltpu.VMEM((rows, channels), bf16),
            pltpu.VMEM((modes, channels), f32),
            pltpu.VMEM((modes, channels), f32),
            pltpu.VMEM((CHUNKS // 2, channels, WIDE), bf16),
            pltpu.VMEM((CHUNKS, rows // 2, WIDE), f32),
            pltpu.VMEM((3 * FORWARDS, rows // 2, WIDE), f32),
            pltpu.VMEM((FORWARDS, rows // 2, WIDE), bf16),
            pltpu.VMEM((rows, channels), bf16),
            pltpu.VMEM((rows * SUB, LANES), f32),
            pltpu.VMEM((rows * SUB, LANES), f32),
            pltpu.VMEM(whole, f32),
            pltpu.VMEM(whole, f32),
            pltpu.VMEM(whole, f32),
            pltpu.VMEM(half, f32),
            pltpu.VMEM(half, f32),
            pltpu.VMEM(half, f32),
            pltpu.VMEM(half, f32),
            pltpu.VMEM((stages - 1,) + half, f32),
            pltpu.VMEM(half, f32),
            pltpu.VMEM(half, f32),
            pltpu.VMEM(half, f32),
            dma((3 + 2 * SLABS,)),
            dma((CHUNKS // 2,)),
            dma((FORWARDS,)),
            dma((3 * FORWARDS,)),
            dma((3 * FORWARDS,)),
            dma((2,)),
            dma((2,)),
            dma((stages - 1,)),
            dma((stages - 1,)),
        ],
        compiler_params=pltpu.CompilerParams(
            collective_id=0, has_side_effects=True, vmem_limit_bytes=64 * 1024 * 1024
        ),
        cost_estimate=pl.CostEstimate(
            flops=2 * rows * channels * 8 * WIDE, bytes_accessed=2 * channels * 8 * WIDE, transcendentals=0
        ),
    )(gate_stream, key_stream, value_stream, residues, decay_rates, out_weight)


def run(*arrays):
    square = lax.axis_size("chan") == 4 and lax.axis_size("ctx") % 2 == 0 and lax.axis_size("ctx") > 2
    fits = arrays[0].shape[1] == SUB * LANES and arrays[5].shape[1] == 8 * WIDE
    return (fused if square and fits else on_device)(*arrays)


def solution(mesh):
    return jax.shard_map(
        run,
        mesh=mesh,
        in_specs=(
            P("ctx", "chan"),
            P("ctx", "chan"),
            P("ctx", "chan"),
            P(None, "chan"),
            P(None, "chan"),
            P("chan", None),
        ),
        out_specs=P("ctx", "chan"),
        check_vma=False,
    )
```

```python
import functools
import math

import jax
import jax.numpy as jnp
from jax import lax
from jax.experimental import pallas as pl
from jax.experimental.pallas import tpu as pltpu
from jax.sharding import PartitionSpec as P

HIGH = lax.Precision.HIGHEST
TWO_PI = 2.0 * math.pi


def swapped(block, axis, distance):
    count = lax.axis_size(axis)
    route = []
    for low in range(count):
        high = low | 1 << distance
        if high != low and high < count:
            route += [(low, high), (high, low)]
    return lax.ppermute(block, axis, route)


def unit_circle(numer, denom):
    angle = TWO_PI * numer.astype(jnp.float32) / denom
    return (jnp.cos(angle), jnp.sin(angle))


def times(ar, ai, br, bi):
    return (ar * br - ai * bi, ar * bi + ai * br)


def dft_matrix(length, inverse):
    index = jnp.arange(length, dtype=jnp.int32)
    cosine, sine = unit_circle(index[:, None] * index[None, :] % length, length)
    if inverse:
        top = jnp.concatenate([cosine, sine], axis=1)
        bottom = jnp.concatenate([-sine, cosine], axis=1)
    else:
        top = jnp.concatenate([cosine, -sine], axis=1)
        bottom = jnp.concatenate([sine, cosine], axis=1)
    return jnp.concatenate([top, bottom], axis=0)


def along_time(real_part, imag_part, matrix):
    rows = real_part.shape[-1]
    stacked = jnp.concatenate([real_part, imag_part], axis=-1)
    result = jnp.dot(stacked, matrix, precision=HIGH)
    return (result[..., :rows], result[..., rows:])


def filter_terms(residues, decay_rates, length):
    lam = jnp.exp(-decay_rates)
    one_less = -jnp.expm1(-decay_rates)
    base = residues * jnp.sqrt(-jnp.expm1(-2.0 * decay_rates))
    tail = jnp.exp(-decay_rates * length)
    return (base, lam, one_less, tail)


def response(freq, total, filt):
    base, lam, one_less, tail = filt
    wrapped = freq % total
    cosine, sine = unit_circle(wrapped, total)
    half_sine = jnp.sin(math.pi * wrapped.astype(jnp.float32) / total)
    parity_sign = 1.0 - 2.0 * (wrapped % 2).astype(jnp.float32)
    resp_r = 0.0
    resp_i = 0.0
    for mode in range(base.shape[0]):
        numer = base[mode] * (1.0 - tail[mode] * parity_sign)
        den_r = one_less[mode] + 2.0 * lam[mode] * half_sine * half_sine
        den_i = lam[mode] * sine
        norm_sq = den_r * den_r + den_i * den_i
        resp_r = resp_r + numer * den_r / norm_sq
        resp_i = resp_i - numer * den_i / norm_sq
    return (resp_r, resp_i)


def spectral(spec_r, spec_i, q_index, filt, big_p, rows):
    total = 2 * big_p * rows
    fsel = jnp.arange(2, dtype=jnp.int32).reshape((2,) + (1,) * (spec_r.ndim - 1))
    freq = 2 * q_index + fsel
    pos = jnp.arange(rows, dtype=jnp.int32)
    cosine, sine = unit_circle(pos * freq % total, total)
    tw_r, tw_i = times(spec_r, spec_i, cosine, -sine)
    full_r, full_i = along_time(tw_r, tw_i, dft_matrix(rows, False))
    resp_r, resp_i = response(freq + 2 * big_p * pos, total, filt)
    prod_r, prod_i = times(full_r, full_i, resp_r, resp_i)
    back_r, back_i = along_time(prod_r, prod_i, dft_matrix(rows, True))
    return times(back_r, back_i, cosine, sine)


def pre_twiddle(mixed, p_index, big_p, shape_f):
    fsel = jnp.arange(2, dtype=jnp.int32).reshape(shape_f)
    cosine, sine = unit_circle(p_index * fsel % (2 * big_p), 2 * big_p)
    return (mixed * cosine, -mixed * sine)


def post_twiddle(spec_r, spec_i, p_index, big_p, rows, shape_f):
    fsel = jnp.arange(2, dtype=jnp.int32).reshape(shape_f)
    cosine, sine = unit_circle(p_index * fsel % (2 * big_p), 2 * big_p)
    return jnp.sum(cosine * spec_r - sine * spec_i, axis=0) / (2.0 * big_p * rows)


def reverse_bits(device, bits):
    result = jnp.zeros_like(device)
    for bit in range(bits):
        result = result | (device >> bit & 1) << bits - 1 - bit
    return result


def butterfly_forward(real_part, imag_part, device, bits):
    for bit in range(bits - 1, -1, -1):
        half = 1 << bit
        place = device % (2 * half)
        upper = place >= half
        other_r, other_i = swapped((real_part, imag_part), "ctx", bit)
        cosine, sine = unit_circle(jnp.where(upper, place - half, 0), 2 * half)
        tw_r, tw_i = times(other_r - real_part, other_i - imag_part, cosine, -sine)
        real_part = jnp.where(upper, tw_r, real_part + other_r)
        imag_part = jnp.where(upper, tw_i, imag_part + other_i)
    return (real_part, imag_part)


def butterfly_inverse(real_part, imag_part, device, bits):
    for bit in range(bits):
        half = 1 << bit
        place = device % (2 * half)
        upper = place >= half
        cosine, sine = unit_circle(jnp.where(upper, place - half, 0), 2 * half)
        tw_r, tw_i = times(real_part, imag_part, cosine, sine)
        send_r = jnp.where(upper, tw_r, real_part)
        send_i = jnp.where(upper, tw_i, imag_part)
        other_r, other_i = swapped((send_r, send_i), "ctx", bit)
        real_part = jnp.where(upper, other_r - tw_r, real_part + other_r)
        imag_part = jnp.where(upper, other_i - tw_i, imag_part + other_i)
    return (real_part, imag_part)


def on_device(gate_stream, key_stream, value_stream, residues, decay_rates, out_weight):
    big_p = lax.axis_size("ctx")
    bits = big_p.bit_length() - 1
    rows = key_stream.shape[0]
    length = float(big_p * rows)
    device = lax.axis_index("ctx")
    mixed = jnp.transpose(key_stream.astype(jnp.float32) * value_stream.astype(jnp.float32))
    base, lam, one_less, tail = filter_terms(residues, decay_rates, length)
    filt = (base[:, :, None], lam[:, :, None], one_less[:, :, None], tail[:, :, None])
    z_r, z_i = pre_twiddle(mixed, device, big_p, (2, 1, 1))
    y_r, y_i = butterfly_forward(z_r, z_i, device, bits)
    q_index = reverse_bits(device, bits)
    u_r, u_i = spectral(y_r, y_i, q_index, filt, big_p, rows)
    v_r, v_i = butterfly_inverse(u_r, u_i, device, bits)
    conv_t = post_twiddle(v_r, v_i, device, big_p, rows, (2, 1, 1))
    conv_rows = jnp.transpose(conv_t)
    gated = (gate_stream.astype(jnp.float32) * conv_rows).astype(jnp.bfloat16)
    partial_terms = jnp.dot(gated, out_weight, preferred_element_type=jnp.float32)
    return lax.psum_scatter(partial_terms, "chan", scatter_dimension=1, tiled=True).astype(
        jnp.bfloat16
    )


MESH = pl.DeviceIdType.MESH
LANES = 128
SUB = 8
WIDE = 512
CHUNKS = 16
FORWARDS = 4
SLABS = 4


def tree_sum(terms):
    while len(terms) > 1:
        pairs = [terms[i] + terms[i + 1] for i in range(0, len(terms) - 1, 2)]
        terms = pairs + terms[len(pairs) * 2 :]
    return terms[0]


def one_minus_exp(u):
    series = u * (1.0 - u / 2.0 * (1.0 - u / 3.0 * (1.0 - u / 4.0 * (1.0 - u / 5.0 * (1.0 - u / 6.0)))))
    return jnp.where(u > 0.25, 1.0 - jnp.exp(-u), series)


def kernel(
    stages,
    gate_hbm, key_hbm, value_hbm, res_hbm, decay_hbm, w_hbm, out,
    gate, key, value, res, decay, wbuf, sbuf, rbuf, gated,
    xs, ys, lam, base, dec, ends, give, chip, peer_end, zbuf, give_state, peer_state, state,
    in_sem, w_sem, chunk_send, chunk_recv, pair_send, pair_recv, z_send, z_recv,
):
    rows = gate.shape[0]
    modes = res.shape[0]
    half_modes = modes // 2
    half_size = half_modes * SUB
    chan = lax.axis_index("chan")
    ctx = lax.axis_index("ctx")
    core = lax.rem(ctx, 2)
    stage = ctx // 2
    x = lax.rem(chan, 2)
    y = chan // 2
    along_x = y * 2 + (1 - x)
    along_y = (1 - y) * 2 + x
    across = (1 - y) * 2 + (1 - x)
    partner = stage * 2 + (1 - core)

    loads = [
        pltpu.make_async_copy(src, dst, in_sem.at[i])
        for i, (src, dst) in enumerate(
            [(decay_hbm, decay), (res_hbm, res), (gate_hbm, gate)]
        )
    ]
    slab = rows // SLABS

    def stream_load(i):
        src, dst = (key_hbm, key) if i % 2 == 0 else (value_hbm, value)
        here = pl.ds(i // 2 * slab, slab)
        return pltpu.make_async_copy(src.at[here, :], dst.at[here, :], in_sem.at[3 + i])

    for i in range(2 * SLABS):
        stream_load(i).start()
    for load in loads[:2]:
        load.start()

    def w_copy(i):
        owner = (across, along_y if i % 2 else along_x, along_x if i % 2 else along_y, chan)[i // 2]
        column = owner * (2 * WIDE) + (i % 2) * WIDE
        return pltpu.make_async_copy(
            w_hbm.at[:, pl.ds(pl.multiple_of(column, WIDE), WIDE)], wbuf.at[i], w_sem.at[i]
        )

    barrier = pltpu.get_barrier_semaphore()
    pl.semaphore_signal(barrier, inc=1, device_id=(along_x, ctx), device_id_type=MESH)
    pl.semaphore_signal(barrier, inc=1, device_id=(along_y, ctx), device_id_type=MESH)
    pl.semaphore_signal(barrier, inc=1, device_id=(chan, partner), device_id_type=MESH)
    for step in range(1, stages):
        other = lax.rem(stage + step, stages) * 2 + core
        pl.semaphore_signal(barrier, inc=1, device_id=(chan, other), device_id_type=MESH)

    loads[0].wait()
    loads[1].wait()
    for b in range(SUB):
        at = pl.ds(b, modes, stride=SUB)
        d = decay[:, b * LANES : (b + 1) * LANES]
        dec[at, :] = d
        lam[at, :] = jnp.exp(-d)
        base[at, :] = res[:, b * LANES : (b + 1) * LANES] * jnp.sqrt(one_minus_exp(2.0 * d))
    for part in range(SLABS):
        stream_load(2 * part).wait()
        stream_load(2 * part + 1).wait()
        here = slice(part * slab, (part + 1) * slab)
        for b in range(SUB):
            cols = slice(b * LANES, (b + 1) * LANES)
            mixed = key[here, cols].astype(jnp.float32) * value[here, cols].astype(jnp.float32)
            xs[pl.ds(part * slab * SUB + b, slab, stride=SUB), :] = mixed
    loads[2].start()
    for i in range(CHUNKS // 2):
        w_copy(i).start()

    def vec(t):
        return pl.ds(pl.multiple_of(t * SUB, SUB), SUB)

    def mode_rows(half, n):
        return pl.ds(pl.multiple_of(half * half_size + n * SUB, SUB), SUB)

    def half_rows(half):
        return pl.ds(pl.multiple_of(half * half_size, half_size), half_size)

    mid = rows // 2

    def end_states(half, dst):
        lams = [lam[mode_rows(half, n), :] for n in range(half_modes)]

        def step(t, carry):
            low, high = carry
            x_low = xs[vec(t), :]
            x_high = xs[vec(t + mid), :]
            low = tuple(l * h + x_low for l, h in zip(lams, low))
            high = tuple(l * h + x_high for l, h in zip(lams, high))
            return (low, high)

        zero = tuple(jnp.zeros((SUB, LANES), jnp.float32) for _ in range(half_modes))
        low, high = lax.fori_loop(0, mid, step, (zero, zero), unroll=4)
        for n in range(half_modes):
            shrink = jnp.exp(dec[mode_rows(half, n), :] * float(-mid))
            dst[n * SUB : (n + 1) * SUB, :] = shrink * low[n] + high[n]

    end_states(1 - core, give)
    pl.semaphore_wait(barrier, 3 + stages - 1)
    send_end = pltpu.make_async_remote_copy(
        src_ref=give, dst_ref=peer_end, send_sem=pair_send.at[0], recv_sem=pair_recv.at[0],
        device_id=(chan, partner), device_id_type=MESH,
    )
    send_end.start()
    end_states(core, ends)
    send_end.wait_recv()

    own_decay = dec[half_rows(core), :]
    span = jnp.exp(own_decay * float(-rows))
    is_first = core == 0
    end_first = jnp.where(is_first, ends[...], peer_end[...])
    end_second = jnp.where(is_first, peer_end[...], ends[...])
    chip[...] = span * end_first + end_second

    def push(step):
        return pltpu.make_async_remote_copy(
            src_ref=chip, dst_ref=zbuf.at[step - 1], send_sem=z_send.at[step - 1], recv_sem=z_recv.at[step - 1],
            device_id=(chan, lax.rem(stage + step, stages) * 2 + core), device_id_type=MESH,
        )

    for step in range(1, stages):
        @pl.when(stage + step < stages)
        def _():
            push(step).start()

    lams = [lam[n * SUB : (n + 1) * SUB, :] for n in range(modes)]
    bases = [base[n * SUB : (n + 1) * SUB, :] for n in range(modes)]

    def local_step(t, hidden):
        now = xs[vec(t), :]
        hidden = tuple(l * h + now for l, h in zip(lams, hidden))
        ys[vec(t), :] = tree_sum([b * h for b, h in zip(bases, hidden)])
        return hidden

    zero = tuple(jnp.zeros((SUB, LANES), jnp.float32) for _ in range(modes))
    lax.fori_loop(0, rows, local_step, zero, unroll=4)

    state[...] = jnp.zeros_like(state)
    for step in range(1, stages):
        @pl.when(stage >= step)
        def _():
            push(step).wait_recv()
            weight = jnp.exp(dec[half_rows(core), :] * float(-2 * rows * (step - 1)))
            state[...] += weight * zbuf[step - 1]

    begin_first = state[...]
    begin_second = span * begin_first + end_first
    give_state[...] = jnp.where(is_first, begin_second, begin_first)
    send_state = pltpu.make_async_remote_copy(
        src_ref=give_state, dst_ref=peer_state, send_sem=pair_send.at[1], recv_sem=pair_recv.at[1],
        device_id=(chan, partner), device_id_type=MESH,
    )
    send_state.start()
    state[...] = jnp.where(is_first, begin_first, begin_second)

    quarter = rows // 4

    def add_state(half, src, part):
        lams = [lam[mode_rows(half, n), :] for n in range(half_modes)]
        start = part * mid
        low, high = [], []
        for n in range(half_modes):
            d = dec[mode_rows(half, n), :]
            first = base[mode_rows(half, n), :] * src[n * SUB : (n + 1) * SUB, :]
            low.append(first * jnp.exp(d * float(-start)) if part else first)
            high.append(first * jnp.exp(d * float(-start - quarter)))

        def step(t, carry):
            low, high = carry
            low = tuple(l * h for l, h in zip(lams, low))
            high = tuple(l * h for l, h in zip(lams, high))
            ys[vec(t + start), :] += tree_sum(list(low))
            ys[vec(t + start + quarter), :] += tree_sum(list(high))
            return (low, high)

        lax.fori_loop(0, quarter, step, (tuple(low), tuple(high)), unroll=4)

    def gate_rows(part):
        here = slice(part * mid, (part + 1) * mid)
        for b in range(SUB):
            cols = slice(b * LANES, (b + 1) * LANES)
            conv = ys[pl.ds(part * mid * SUB + b, mid, stride=SUB), :]
            gated[here, cols] = (gate[here, cols].astype(jnp.float32) * conv).astype(jnp.bfloat16)

    def chunk_copy(i, target):
        return pltpu.make_async_remote_copy(
            src_ref=sbuf.at[i], dst_ref=rbuf.at[i], send_sem=chunk_send.at[i], recv_sem=chunk_recv.at[i],
            device_id=(target, ctx), device_id_type=MESH,
        )

    def first_target(i):
        odd = lax.rem(i, 2)
        return along_x * (1 - odd) + along_y * odd

    def second_target(i):
        odd = lax.rem(i, 2)
        return along_y * (1 - odd) + along_x * odd

    def w_wait(i):
        pltpu.make_async_copy(w_hbm.at[:, pl.ds(0, WIDE)], wbuf.at[i], w_sem.at[i]).wait()

    def block_of(i):
        return i // 4 * 2 + lax.rem(i, 2)

    def partial_sum(i):
        part = lax.rem(i // 2, 2)
        here = pl.ds(pl.multiple_of(part * mid, mid), mid)
        sbuf[i] = jnp.dot(gated[here, :], wbuf[block_of(i)], preferred_element_type=jnp.float32)

    add_state(core, state, 0)
    send_state.wait_recv()
    add_state(1 - core, peer_state, 0)
    loads[2].wait()
    gate_rows(0)

    @pl.loop(0, 2)
    def _(i):
        w_wait(i)
        partial_sum(i)
        chunk_copy(i, first_target(i)).start()

    add_state(core, state, 1)
    add_state(1 - core, peer_state, 1)
    gate_rows(1)

    @pl.loop(2, CHUNKS)
    def _(i):
        @pl.when(lax.rem(i // 2, 2) == 0)
        def _():
            w_wait(block_of(i))

        partial_sum(i)

        @pl.when(i < FORWARDS)
        def _():
            chunk_copy(i, first_target(i)).start()

    @pl.loop(0, FORWARDS)
    def _(j):
        chunk_copy(j, first_target(j)).wait_send()
        chunk_copy(j + FORWARDS, first_target(j)).start()

    @pl.loop(0, FORWARDS)
    def _(j):
        chunk_copy(j, first_target(j)).wait_recv()
        sbuf[j + 2 * FORWARDS] += rbuf[j]
        chunk_copy(j + 2 * FORWARDS, second_target(j)).start()

    @pl.loop(0, FORWARDS)
    def _(j):
        chunk_copy(j + FORWARDS, first_target(j)).wait_recv()
        sbuf[j + 3 * FORWARDS] += rbuf[j + FORWARDS]

    @pl.loop(0, FORWARDS)
    def _(j):
        chunk_copy(j + 2 * FORWARDS, second_target(j)).wait_recv()
        here = pl.ds(pl.multiple_of(j // 2 * mid, mid), mid)
        cols = pl.ds(pl.multiple_of(lax.rem(j, 2) * WIDE, WIDE), WIDE)
        out[here, cols] = (sbuf[j + 3 * FORWARDS] + rbuf[j + 2 * FORWARDS]).astype(jnp.bfloat16)

    send_end.wait_send()
    send_state.wait_send()
    for step in range(1, stages):
        @pl.when(stage + step < stages)
        def _():
            push(step).wait_send()

    @pl.loop(0, FORWARDS)
    def _(j):
        chunk_copy(j + FORWARDS, first_target(j)).wait_send()
        chunk_copy(j + 2 * FORWARDS, second_target(j)).wait_send()


def fused(gate_stream, key_stream, value_stream, residues, decay_rates, out_weight):
    rows, channels = gate_stream.shape
    modes = residues.shape[0]
    stages = lax.axis_size("ctx") // 2
    f32, bf16 = jnp.float32, jnp.bfloat16
    whole = (modes * SUB, LANES)
    half = (modes // 2 * SUB, LANES)
    dma = pltpu.SemaphoreType.DMA
    return pl.pallas_call(
        functools.partial(kernel, stages),
        out_shape=pltpu.VMEM((rows, 2 * WIDE), bf16),
        in_specs=[pl.BlockSpec(memory_space=pltpu.HBM)] * 6,
        out_specs=pl.BlockSpec(memory_space=pltpu.VMEM),
        scratch_shapes=[
            pltpu.VMEM((rows, channels), bf16),
            pltpu.VMEM((rows, channels), bf16),
            pltpu.VMEM((rows, channels), bf16),
            pltpu.VMEM((modes, channels), f32),
            pltpu.VMEM((modes, channels), f32),
            pltpu.VMEM((CHUNKS // 2, channels, WIDE), bf16),
            pltpu.VMEM((CHUNKS, rows // 2, WIDE), f32),
            pltpu.VMEM((3 * FORWARDS, rows // 2, WIDE), f32),
            pltpu.VMEM((rows, channels), bf16),
            pltpu.VMEM((rows * SUB, LANES), f32),
            pltpu.VMEM((rows * SUB, LANES), f32),
            pltpu.VMEM(whole, f32),
            pltpu.VMEM(whole, f32),
            pltpu.VMEM(whole, f32),
            pltpu.VMEM(half, f32),
            pltpu.VMEM(half, f32),
            pltpu.VMEM(half, f32),
            pltpu.VMEM(half, f32),
            pltpu.VMEM((stages - 1,) + half, f32),
            pltpu.VMEM(half, f32),
            pltpu.VMEM(half, f32),
            pltpu.VMEM(half, f32),
            dma((3 + 2 * SLABS,)),
            dma((CHUNKS // 2,)),
            dma((3 * FORWARDS,)),
            dma((3 * FORWARDS,)),
            dma((2,)),
            dma((2,)),
            dma((stages - 1,)),
            dma((stages - 1,)),
        ],
        compiler_params=pltpu.CompilerParams(
            collective_id=0, has_side_effects=True, vmem_limit_bytes=63 * 1024 * 1024
        ),
        cost_estimate=pl.CostEstimate(
            flops=2 * rows * channels * 8 * WIDE, bytes_accessed=2 * channels * 8 * WIDE, transcendentals=0
        ),
    )(gate_stream, key_stream, value_stream, residues, decay_rates, out_weight)


def run(*arrays):
    square = lax.axis_size("chan") == 4 and lax.axis_size("ctx") % 2 == 0 and lax.axis_size("ctx") > 2
    fits = arrays[0].shape[1] == SUB * LANES and arrays[5].shape[1] == 8 * WIDE
    return (fused if square and fits else on_device)(*arrays)


def solution(mesh):
    return jax.shard_map(
        run,
        mesh=mesh,
        in_specs=(
            P("ctx", "chan"),
            P("ctx", "chan"),
            P("ctx", "chan"),
            P(None, "chan"),
            P(None, "chan"),
            P("chan", None),
        ),
        out_specs=P("ctx", "chan"),
        check_vma=False,
    )
```

```python
import functools
import math

import jax
import jax.numpy as jnp
from jax import lax
from jax.experimental import pallas as pl
from jax.experimental.pallas import tpu as pltpu
from jax.sharding import PartitionSpec as P

HIGH = lax.Precision.HIGHEST
TWO_PI = 2.0 * math.pi


def swapped(block, axis, distance):
    count = lax.axis_size(axis)
    route = []
    for low in range(count):
        high = low | 1 << distance
        if high != low and high < count:
            route += [(low, high), (high, low)]
    return lax.ppermute(block, axis, route)


def unit_circle(numer, denom):
    angle = TWO_PI * numer.astype(jnp.float32) / denom
    return (jnp.cos(angle), jnp.sin(angle))


def times(ar, ai, br, bi):
    return (ar * br - ai * bi, ar * bi + ai * br)


def dft_matrix(length, inverse):
    index = jnp.arange(length, dtype=jnp.int32)
    cosine, sine = unit_circle(index[:, None] * index[None, :] % length, length)
    if inverse:
        top = jnp.concatenate([cosine, sine], axis=1)
        bottom = jnp.concatenate([-sine, cosine], axis=1)
    else:
        top = jnp.concatenate([cosine, -sine], axis=1)
        bottom = jnp.concatenate([sine, cosine], axis=1)
    return jnp.concatenate([top, bottom], axis=0)


def along_time(real_part, imag_part, matrix):
    rows = real_part.shape[-1]
    stacked = jnp.concatenate([real_part, imag_part], axis=-1)
    result = jnp.dot(stacked, matrix, precision=HIGH)
    return (result[..., :rows], result[..., rows:])


def filter_terms(residues, decay_rates, length):
    lam = jnp.exp(-decay_rates)
    one_less = -jnp.expm1(-decay_rates)
    base = residues * jnp.sqrt(-jnp.expm1(-2.0 * decay_rates))
    tail = jnp.exp(-decay_rates * length)
    return (base, lam, one_less, tail)


def response(freq, total, filt):
    base, lam, one_less, tail = filt
    wrapped = freq % total
    cosine, sine = unit_circle(wrapped, total)
    half_sine = jnp.sin(math.pi * wrapped.astype(jnp.float32) / total)
    parity_sign = 1.0 - 2.0 * (wrapped % 2).astype(jnp.float32)
    resp_r = 0.0
    resp_i = 0.0
    for mode in range(base.shape[0]):
        numer = base[mode] * (1.0 - tail[mode] * parity_sign)
        den_r = one_less[mode] + 2.0 * lam[mode] * half_sine * half_sine
        den_i = lam[mode] * sine
        norm_sq = den_r * den_r + den_i * den_i
        resp_r = resp_r + numer * den_r / norm_sq
        resp_i = resp_i - numer * den_i / norm_sq
    return (resp_r, resp_i)


def spectral(spec_r, spec_i, q_index, filt, big_p, rows):
    total = 2 * big_p * rows
    fsel = jnp.arange(2, dtype=jnp.int32).reshape((2,) + (1,) * (spec_r.ndim - 1))
    freq = 2 * q_index + fsel
    pos = jnp.arange(rows, dtype=jnp.int32)
    cosine, sine = unit_circle(pos * freq % total, total)
    tw_r, tw_i = times(spec_r, spec_i, cosine, -sine)
    full_r, full_i = along_time(tw_r, tw_i, dft_matrix(rows, False))
    resp_r, resp_i = response(freq + 2 * big_p * pos, total, filt)
    prod_r, prod_i = times(full_r, full_i, resp_r, resp_i)
    back_r, back_i = along_time(prod_r, prod_i, dft_matrix(rows, True))
    return times(back_r, back_i, cosine, sine)


def pre_twiddle(mixed, p_index, big_p, shape_f):
    fsel = jnp.arange(2, dtype=jnp.int32).reshape(shape_f)
    cosine, sine = unit_circle(p_index * fsel % (2 * big_p), 2 * big_p)
    return (mixed * cosine, -mixed * sine)


def post_twiddle(spec_r, spec_i, p_index, big_p, rows, shape_f):
    fsel = jnp.arange(2, dtype=jnp.int32).reshape(shape_f)
    cosine, sine = unit_circle(p_index * fsel % (2 * big_p), 2 * big_p)
    return jnp.sum(cosine * spec_r - sine * spec_i, axis=0) / (2.0 * big_p * rows)


def reverse_bits(device, bits):
    result = jnp.zeros_like(device)
    for bit in range(bits):
        result = result | (device >> bit & 1) << bits - 1 - bit
    return result


def butterfly_forward(real_part, imag_part, device, bits):
    for bit in range(bits - 1, -1, -1):
        half = 1 << bit
        place = device % (2 * half)
        upper = place >= half
        other_r, other_i = swapped((real_part, imag_part), "ctx", bit)
        cosine, sine = unit_circle(jnp.where(upper, place - half, 0), 2 * half)
        tw_r, tw_i = times(other_r - real_part, other_i - imag_part, cosine, -sine)
        real_part = jnp.where(upper, tw_r, real_part + other_r)
        imag_part = jnp.where(upper, tw_i, imag_part + other_i)
    return (real_part, imag_part)


def butterfly_inverse(real_part, imag_part, device, bits):
    for bit in range(bits):
        half = 1 << bit
        place = device % (2 * half)
        upper = place >= half
        cosine, sine = unit_circle(jnp.where(upper, place - half, 0), 2 * half)
        tw_r, tw_i = times(real_part, imag_part, cosine, sine)
        send_r = jnp.where(upper, tw_r, real_part)
        send_i = jnp.where(upper, tw_i, imag_part)
        other_r, other_i = swapped((send_r, send_i), "ctx", bit)
        real_part = jnp.where(upper, other_r - tw_r, real_part + other_r)
        imag_part = jnp.where(upper, other_i - tw_i, imag_part + other_i)
    return (real_part, imag_part)


def on_device(gate_stream, key_stream, value_stream, residues, decay_rates, out_weight):
    big_p = lax.axis_size("ctx")
    bits = big_p.bit_length() - 1
    rows = key_stream.shape[0]
    length = float(big_p * rows)
    device = lax.axis_index("ctx")
    mixed = jnp.transpose(key_stream.astype(jnp.float32) * value_stream.astype(jnp.float32))
    base, lam, one_less, tail = filter_terms(residues, decay_rates, length)
    filt = (base[:, :, None], lam[:, :, None], one_less[:, :, None], tail[:, :, None])
    z_r, z_i = pre_twiddle(mixed, device, big_p, (2, 1, 1))
    y_r, y_i = butterfly_forward(z_r, z_i, device, bits)
    q_index = reverse_bits(device, bits)
    u_r, u_i = spectral(y_r, y_i, q_index, filt, big_p, rows)
    v_r, v_i = butterfly_inverse(u_r, u_i, device, bits)
    conv_t = post_twiddle(v_r, v_i, device, big_p, rows, (2, 1, 1))
    conv_rows = jnp.transpose(conv_t)
    gated = (gate_stream.astype(jnp.float32) * conv_rows).astype(jnp.bfloat16)
    partial_terms = jnp.dot(gated, out_weight, preferred_element_type=jnp.float32)
    return lax.psum_scatter(partial_terms, "chan", scatter_dimension=1, tiled=True).astype(
        jnp.bfloat16
    )


MESH = pl.DeviceIdType.MESH
LANES = 128
SUB = 8
WIDE = 512
CHUNKS = 16
FORWARDS = 4
SLABS = 4


def tree_sum(terms):
    while len(terms) > 1:
        pairs = [terms[i] + terms[i + 1] for i in range(0, len(terms) - 1, 2)]
        terms = pairs + terms[len(pairs) * 2 :]
    return terms[0]


def one_minus_exp(u):
    series = u * (1.0 - u / 2.0 * (1.0 - u / 3.0 * (1.0 - u / 4.0 * (1.0 - u / 5.0 * (1.0 - u / 6.0)))))
    return jnp.where(u > 0.25, 1.0 - jnp.exp(-u), series)


def kernel(
    stages,
    gate_hbm, key_hbm, value_hbm, res_hbm, decay_hbm, w_hbm, out,
    gate, key, value, res, decay, wbuf, sbuf, rbuf, gated,
    xs, ys, lam, base, dec, carried, ends, give, chip, peer_end, zbuf, give_state, peer_state, state,
    in_sem, w_sem, chunk_send, chunk_recv, pair_send, pair_recv, z_send, z_recv,
):
    rows = gate.shape[0]
    modes = res.shape[0]
    half_modes = modes // 2
    half_size = half_modes * SUB
    chan = lax.axis_index("chan")
    ctx = lax.axis_index("ctx")
    core = lax.rem(ctx, 2)
    stage = ctx // 2
    x = lax.rem(chan, 2)
    y = chan // 2
    along_x = y * 2 + (1 - x)
    along_y = (1 - y) * 2 + x
    across = (1 - y) * 2 + (1 - x)
    partner = stage * 2 + (1 - core)

    loads = [
        pltpu.make_async_copy(src, dst, in_sem.at[i])
        for i, (src, dst) in enumerate(
            [(decay_hbm, decay), (res_hbm, res), (gate_hbm, gate)]
        )
    ]
    slab = rows // SLABS

    def stream_load(i):
        src, dst = (key_hbm, key) if i % 2 == 0 else (value_hbm, value)
        here = pl.ds(i // 2 * slab, slab)
        return pltpu.make_async_copy(src.at[here, :], dst.at[here, :], in_sem.at[3 + i])

    for i in range(2 * SLABS):
        stream_load(i).start()
    for load in loads[:2]:
        load.start()

    def w_copy(i):
        owner = (across, along_y if i % 2 else along_x, along_x if i % 2 else along_y, chan)[i // 2]
        column = owner * (2 * WIDE) + (i % 2) * WIDE
        return pltpu.make_async_copy(
            w_hbm.at[:, pl.ds(pl.multiple_of(column, WIDE), WIDE)], wbuf.at[i], w_sem.at[i]
        )

    barrier = pltpu.get_barrier_semaphore()
    pl.semaphore_signal(barrier, inc=1, device_id=(along_x, ctx), device_id_type=MESH)
    pl.semaphore_signal(barrier, inc=1, device_id=(along_y, ctx), device_id_type=MESH)
    pl.semaphore_signal(barrier, inc=1, device_id=(chan, partner), device_id_type=MESH)
    for step in range(1, stages):
        other = lax.rem(stage + step, stages) * 2 + core
        pl.semaphore_signal(barrier, inc=1, device_id=(chan, other), device_id_type=MESH)

    loads[0].wait()
    loads[1].wait()
    for b in range(SUB):
        at = pl.ds(b, modes, stride=SUB)
        d = decay[:, b * LANES : (b + 1) * LANES]
        dec[at, :] = d
        lam[at, :] = jnp.exp(-d)
        base[at, :] = res[:, b * LANES : (b + 1) * LANES] * jnp.sqrt(one_minus_exp(2.0 * d))
    for part in range(SLABS):
        stream_load(2 * part).wait()
        stream_load(2 * part + 1).wait()
        here = slice(part * slab, (part + 1) * slab)
        for b in range(SUB):
            cols = slice(b * LANES, (b + 1) * LANES)
            mixed = key[here, cols].astype(jnp.float32) * value[here, cols].astype(jnp.float32)
            xs[pl.ds(part * slab * SUB + b, slab, stride=SUB), :] = mixed
    loads[2].start()
    for i in range(CHUNKS // 2):
        w_copy(i).start()

    def vec(t):
        return pl.ds(pl.multiple_of(t * SUB, SUB), SUB)

    def mode_rows(half, n):
        return pl.ds(pl.multiple_of(half * half_size + n * SUB, SUB), SUB)

    def half_rows(half):
        return pl.ds(pl.multiple_of(half * half_size, half_size), half_size)

    mid = rows // 2

    def end_states(half, dst):
        lams = [lam[mode_rows(half, n), :] for n in range(half_modes)]

        def step(t, carry):
            low, high = carry
            x_low = xs[vec(t), :]
            x_high = xs[vec(t + mid), :]
            low = tuple(l * h + x_low for l, h in zip(lams, low))
            high = tuple(l * h + x_high for l, h in zip(lams, high))
            return (low, high)

        zero = tuple(jnp.zeros((SUB, LANES), jnp.float32) for _ in range(half_modes))
        low, high = lax.fori_loop(0, mid, step, (zero, zero), unroll=4)
        for n in range(half_modes):
            shrink = jnp.exp(dec[mode_rows(half, n), :] * float(-mid))
            dst[n * SUB : (n + 1) * SUB, :] = shrink * low[n] + high[n]

    end_states(1 - core, give)
    pl.semaphore_wait(barrier, 3 + stages - 1)
    send_end = pltpu.make_async_remote_copy(
        src_ref=give, dst_ref=peer_end, send_sem=pair_send.at[0], recv_sem=pair_recv.at[0],
        device_id=(chan, partner), device_id_type=MESH,
    )
    send_end.start()
    end_states(core, ends)
    send_end.wait_recv()

    own_decay = dec[half_rows(core), :]
    span = jnp.exp(own_decay * float(-rows))
    is_first = core == 0
    end_first = jnp.where(is_first, ends[...], peer_end[...])
    end_second = jnp.where(is_first, peer_end[...], ends[...])
    chip[...] = span * end_first + end_second

    def push(step):
        return pltpu.make_async_remote_copy(
            src_ref=chip, dst_ref=zbuf.at[step - 1], send_sem=z_send.at[step - 1], recv_sem=z_recv.at[step - 1],
            device_id=(chan, lax.rem(stage + step, stages) * 2 + core), device_id_type=MESH,
        )

    for step in range(1, stages):
        @pl.when(stage + step < stages)
        def _():
            push(step).start()

    def local_rows(part):
        lams = [lam[n * SUB : (n + 1) * SUB, :] for n in range(modes)]
        bases = [base[n * SUB : (n + 1) * SUB, :] for n in range(modes)]

        def step(t, hidden):
            now = xs[vec(t), :]
            hidden = tuple(l * h + now for l, h in zip(lams, hidden))
            ys[vec(t), :] = tree_sum([b * h for b, h in zip(bases, hidden)])
            return hidden

        if part:
            start = tuple(carried[n * SUB : (n + 1) * SUB, :] for n in range(modes))
        else:
            start = tuple(jnp.zeros((SUB, LANES), jnp.float32) for _ in range(modes))
        hidden = lax.fori_loop(part * mid, (part + 1) * mid, step, start, unroll=4)
        if not part:
            for n in range(modes):
                carried[n * SUB : (n + 1) * SUB, :] = hidden[n]

    local_rows(0)
    state[...] = jnp.zeros_like(state)
    for step in range(1, stages):
        @pl.when(stage >= step)
        def _():
            push(step).wait_recv()
            weight = jnp.exp(dec[half_rows(core), :] * float(-2 * rows * (step - 1)))
            state[...] += weight * zbuf[step - 1]

    begin_first = state[...]
    begin_second = span * begin_first + end_first
    give_state[...] = jnp.where(is_first, begin_second, begin_first)
    send_state = pltpu.make_async_remote_copy(
        src_ref=give_state, dst_ref=peer_state, send_sem=pair_send.at[1], recv_sem=pair_recv.at[1],
        device_id=(chan, partner), device_id_type=MESH,
    )
    send_state.start()
    state[...] = jnp.where(is_first, begin_first, begin_second)

    quarter = rows // 4

    def add_state(half, src, part):
        lams = [lam[mode_rows(half, n), :] for n in range(half_modes)]
        start = part * mid
        low, high = [], []
        for n in range(half_modes):
            d = dec[mode_rows(half, n), :]
            first = base[mode_rows(half, n), :] * src[n * SUB : (n + 1) * SUB, :]
            low.append(first * jnp.exp(d * float(-start)) if part else first)
            high.append(first * jnp.exp(d * float(-start - quarter)))

        def step(t, carry):
            low, high = carry
            low = tuple(l * h for l, h in zip(lams, low))
            high = tuple(l * h for l, h in zip(lams, high))
            ys[vec(t + start), :] += tree_sum(list(low))
            ys[vec(t + start + quarter), :] += tree_sum(list(high))
            return (low, high)

        lax.fori_loop(0, quarter, step, (tuple(low), tuple(high)), unroll=4)

    def gate_rows(part):
        here = slice(part * mid, (part + 1) * mid)
        for b in range(SUB):
            cols = slice(b * LANES, (b + 1) * LANES)
            conv = ys[pl.ds(part * mid * SUB + b, mid, stride=SUB), :]
            gated[here, cols] = (gate[here, cols].astype(jnp.float32) * conv).astype(jnp.bfloat16)

    def chunk_copy(i, target):
        return pltpu.make_async_remote_copy(
            src_ref=sbuf.at[i], dst_ref=rbuf.at[i], send_sem=chunk_send.at[i], recv_sem=chunk_recv.at[i],
            device_id=(target, ctx), device_id_type=MESH,
        )

    def first_target(i):
        odd = lax.rem(i, 2)
        return along_x * (1 - odd) + along_y * odd

    def second_target(i):
        odd = lax.rem(i, 2)
        return along_y * (1 - odd) + along_x * odd

    def w_wait(i):
        pltpu.make_async_copy(w_hbm.at[:, pl.ds(0, WIDE)], wbuf.at[i], w_sem.at[i]).wait()

    def block_of(i):
        return i // 4 * 2 + lax.rem(i, 2)

    def partial_sum(i):
        part = lax.rem(i // 2, 2)
        here = pl.ds(pl.multiple_of(part * mid, mid), mid)
        sbuf[i] = jnp.dot(gated[here, :], wbuf[block_of(i)], preferred_element_type=jnp.float32)

    add_state(core, state, 0)
    send_state.wait_recv()
    add_state(1 - core, peer_state, 0)
    loads[2].wait()
    gate_rows(0)

    @pl.loop(0, 2)
    def _(i):
        w_wait(i)
        partial_sum(i)
        chunk_copy(i, first_target(i)).start()

    local_rows(1)
    add_state(core, state, 1)
    add_state(1 - core, peer_state, 1)
    gate_rows(1)

    @pl.loop(2, CHUNKS)
    def _(i):
        @pl.when(lax.rem(i // 2, 2) == 0)
        def _():
            w_wait(block_of(i))

        partial_sum(i)

        @pl.when(i < FORWARDS)
        def _():
            chunk_copy(i, first_target(i)).start()

    @pl.loop(0, FORWARDS)
    def _(j):
        chunk_copy(j, first_target(j)).wait_send()
        chunk_copy(j + FORWARDS, first_target(j)).start()

    @pl.loop(0, FORWARDS)
    def _(j):
        chunk_copy(j, first_target(j)).wait_recv()
        sbuf[j + 2 * FORWARDS] += rbuf[j]
        chunk_copy(j + 2 * FORWARDS, second_target(j)).start()

    @pl.loop(0, FORWARDS)
    def _(j):
        chunk_copy(j + FORWARDS, first_target(j)).wait_recv()
        sbuf[j + 3 * FORWARDS] += rbuf[j + FORWARDS]

    @pl.loop(0, FORWARDS)
    def _(j):
        chunk_copy(j + 2 * FORWARDS, second_target(j)).wait_recv()
        here = pl.ds(pl.multiple_of(j // 2 * mid, mid), mid)
        cols = pl.ds(pl.multiple_of(lax.rem(j, 2) * WIDE, WIDE), WIDE)
        out[here, cols] = (sbuf[j + 3 * FORWARDS] + rbuf[j + 2 * FORWARDS]).astype(jnp.bfloat16)

    send_end.wait_send()
    send_state.wait_send()
    for step in range(1, stages):
        @pl.when(stage + step < stages)
        def _():
            push(step).wait_send()

    @pl.loop(0, FORWARDS)
    def _(j):
        chunk_copy(j + FORWARDS, first_target(j)).wait_send()
        chunk_copy(j + 2 * FORWARDS, second_target(j)).wait_send()


def fused(gate_stream, key_stream, value_stream, residues, decay_rates, out_weight):
    rows, channels = gate_stream.shape
    modes = residues.shape[0]
    stages = lax.axis_size("ctx") // 2
    f32, bf16 = jnp.float32, jnp.bfloat16
    whole = (modes * SUB, LANES)
    half = (modes // 2 * SUB, LANES)
    dma = pltpu.SemaphoreType.DMA
    return pl.pallas_call(
        functools.partial(kernel, stages),
        out_shape=pltpu.VMEM((rows, 2 * WIDE), bf16),
        in_specs=[pl.BlockSpec(memory_space=pltpu.HBM)] * 6,
        out_specs=pl.BlockSpec(memory_space=pltpu.VMEM),
        scratch_shapes=[
            pltpu.VMEM((rows, channels), bf16),
            pltpu.VMEM((rows, channels), bf16),
            pltpu.VMEM((rows, channels), bf16),
            pltpu.VMEM((modes, channels), f32),
            pltpu.VMEM((modes, channels), f32),
            pltpu.VMEM((CHUNKS // 2, channels, WIDE), bf16),
            pltpu.VMEM((CHUNKS, rows // 2, WIDE), f32),
            pltpu.VMEM((3 * FORWARDS, rows // 2, WIDE), f32),
            pltpu.VMEM((rows, channels), bf16),
            pltpu.VMEM((rows * SUB, LANES), f32),
            pltpu.VMEM((rows * SUB, LANES), f32),
            pltpu.VMEM(whole, f32),
            pltpu.VMEM(whole, f32),
            pltpu.VMEM(whole, f32),
            pltpu.VMEM(whole, f32),
            pltpu.VMEM(half, f32),
            pltpu.VMEM(half, f32),
            pltpu.VMEM(half, f32),
            pltpu.VMEM(half, f32),
            pltpu.VMEM((stages - 1,) + half, f32),
            pltpu.VMEM(half, f32),
            pltpu.VMEM(half, f32),
            pltpu.VMEM(half, f32),
            dma((3 + 2 * SLABS,)),
            dma((CHUNKS // 2,)),
            dma((3 * FORWARDS,)),
            dma((3 * FORWARDS,)),
            dma((2,)),
            dma((2,)),
            dma((stages - 1,)),
            dma((stages - 1,)),
        ],
        compiler_params=pltpu.CompilerParams(
            collective_id=0, has_side_effects=True, vmem_limit_bytes=63 * 1024 * 1024
        ),
        cost_estimate=pl.CostEstimate(
            flops=2 * rows * channels * 8 * WIDE, bytes_accessed=2 * channels * 8 * WIDE, transcendentals=0
        ),
    )(gate_stream, key_stream, value_stream, residues, decay_rates, out_weight)


def run(*arrays):
    square = lax.axis_size("chan") == 4 and lax.axis_size("ctx") % 2 == 0 and lax.axis_size("ctx") > 2
    fits = arrays[0].shape[1] == SUB * LANES and arrays[5].shape[1] == 8 * WIDE
    return (fused if square and fits else on_device)(*arrays)


def solution(mesh):
    return jax.shard_map(
        run,
        mesh=mesh,
        in_specs=(
            P("ctx", "chan"),
            P("ctx", "chan"),
            P("ctx", "chan"),
            P(None, "chan"),
            P(None, "chan"),
            P("chan", None),
        ),
        out_specs=P("ctx", "chan"),
        check_vma=False,
    )
```

```python
import functools
import math

import jax
import jax.numpy as jnp
from jax import lax
from jax.experimental import pallas as pl
from jax.experimental.pallas import tpu as pltpu
from jax.sharding import PartitionSpec as P

HIGH = lax.Precision.HIGHEST
TWO_PI = 2.0 * math.pi


def swapped(block, axis, distance):
    count = lax.axis_size(axis)
    route = []
    for low in range(count):
        high = low | 1 << distance
        if high != low and high < count:
            route += [(low, high), (high, low)]
    return lax.ppermute(block, axis, route)


def unit_circle(numer, denom):
    angle = TWO_PI * numer.astype(jnp.float32) / denom
    return (jnp.cos(angle), jnp.sin(angle))


def times(ar, ai, br, bi):
    return (ar * br - ai * bi, ar * bi + ai * br)


def dft_matrix(length, inverse):
    index = jnp.arange(length, dtype=jnp.int32)
    cosine, sine = unit_circle(index[:, None] * index[None, :] % length, length)
    if inverse:
        top = jnp.concatenate([cosine, sine], axis=1)
        bottom = jnp.concatenate([-sine, cosine], axis=1)
    else:
        top = jnp.concatenate([cosine, -sine], axis=1)
        bottom = jnp.concatenate([sine, cosine], axis=1)
    return jnp.concatenate([top, bottom], axis=0)


def along_time(real_part, imag_part, matrix):
    rows = real_part.shape[-1]
    stacked = jnp.concatenate([real_part, imag_part], axis=-1)
    result = jnp.dot(stacked, matrix, precision=HIGH)
    return (result[..., :rows], result[..., rows:])


def filter_terms(residues, decay_rates, length):
    lam = jnp.exp(-decay_rates)
    one_less = -jnp.expm1(-decay_rates)
    base = residues * jnp.sqrt(-jnp.expm1(-2.0 * decay_rates))
    tail = jnp.exp(-decay_rates * length)
    return (base, lam, one_less, tail)


def response(freq, total, filt):
    base, lam, one_less, tail = filt
    wrapped = freq % total
    cosine, sine = unit_circle(wrapped, total)
    half_sine = jnp.sin(math.pi * wrapped.astype(jnp.float32) / total)
    parity_sign = 1.0 - 2.0 * (wrapped % 2).astype(jnp.float32)
    resp_r = 0.0
    resp_i = 0.0
    for mode in range(base.shape[0]):
        numer = base[mode] * (1.0 - tail[mode] * parity_sign)
        den_r = one_less[mode] + 2.0 * lam[mode] * half_sine * half_sine
        den_i = lam[mode] * sine
        norm_sq = den_r * den_r + den_i * den_i
        resp_r = resp_r + numer * den_r / norm_sq
        resp_i = resp_i - numer * den_i / norm_sq
    return (resp_r, resp_i)


def spectral(spec_r, spec_i, q_index, filt, big_p, rows):
    total = 2 * big_p * rows
    fsel = jnp.arange(2, dtype=jnp.int32).reshape((2,) + (1,) * (spec_r.ndim - 1))
    freq = 2 * q_index + fsel
    pos = jnp.arange(rows, dtype=jnp.int32)
    cosine, sine = unit_circle(pos * freq % total, total)
    tw_r, tw_i = times(spec_r, spec_i, cosine, -sine)
    full_r, full_i = along_time(tw_r, tw_i, dft_matrix(rows, False))
    resp_r, resp_i = response(freq + 2 * big_p * pos, total, filt)
    prod_r, prod_i = times(full_r, full_i, resp_r, resp_i)
    back_r, back_i = along_time(prod_r, prod_i, dft_matrix(rows, True))
    return times(back_r, back_i, cosine, sine)


def pre_twiddle(mixed, p_index, big_p, shape_f):
    fsel = jnp.arange(2, dtype=jnp.int32).reshape(shape_f)
    cosine, sine = unit_circle(p_index * fsel % (2 * big_p), 2 * big_p)
    return (mixed * cosine, -mixed * sine)


def post_twiddle(spec_r, spec_i, p_index, big_p, rows, shape_f):
    fsel = jnp.arange(2, dtype=jnp.int32).reshape(shape_f)
    cosine, sine = unit_circle(p_index * fsel % (2 * big_p), 2 * big_p)
    return jnp.sum(cosine * spec_r - sine * spec_i, axis=0) / (2.0 * big_p * rows)


def reverse_bits(device, bits):
    result = jnp.zeros_like(device)
    for bit in range(bits):
        result = result | (device >> bit & 1) << bits - 1 - bit
    return result


def butterfly_forward(real_part, imag_part, device, bits):
    for bit in range(bits - 1, -1, -1):
        half = 1 << bit
        place = device % (2 * half)
        upper = place >= half
        other_r, other_i = swapped((real_part, imag_part), "ctx", bit)
        cosine, sine = unit_circle(jnp.where(upper, place - half, 0), 2 * half)
        tw_r, tw_i = times(other_r - real_part, other_i - imag_part, cosine, -sine)
        real_part = jnp.where(upper, tw_r, real_part + other_r)
        imag_part = jnp.where(upper, tw_i, imag_part + other_i)
    return (real_part, imag_part)


def butterfly_inverse(real_part, imag_part, device, bits):
    for bit in range(bits):
        half = 1 << bit
        place = device % (2 * half)
        upper = place >= half
        cosine, sine = unit_circle(jnp.where(upper, place - half, 0), 2 * half)
        tw_r, tw_i = times(real_part, imag_part, cosine, sine)
        send_r = jnp.where(upper, tw_r, real_part)
        send_i = jnp.where(upper, tw_i, imag_part)
        other_r, other_i = swapped((send_r, send_i), "ctx", bit)
        real_part = jnp.where(upper, other_r - tw_r, real_part + other_r)
        imag_part = jnp.where(upper, other_i - tw_i, imag_part + other_i)
    return (real_part, imag_part)


def on_device(gate_stream, key_stream, value_stream, residues, decay_rates, out_weight):
    big_p = lax.axis_size("ctx")
    bits = big_p.bit_length() - 1
    rows = key_stream.shape[0]
    length = float(big_p * rows)
    device = lax.axis_index("ctx")
    mixed = jnp.transpose(key_stream.astype(jnp.float32) * value_stream.astype(jnp.float32))
    base, lam, one_less, tail = filter_terms(residues, decay_rates, length)
    filt = (base[:, :, None], lam[:, :, None], one_less[:, :, None], tail[:, :, None])
    z_r, z_i = pre_twiddle(mixed, device, big_p, (2, 1, 1))
    y_r, y_i = butterfly_forward(z_r, z_i, device, bits)
    q_index = reverse_bits(device, bits)
    u_r, u_i = spectral(y_r, y_i, q_index, filt, big_p, rows)
    v_r, v_i = butterfly_inverse(u_r, u_i, device, bits)
    conv_t = post_twiddle(v_r, v_i, device, big_p, rows, (2, 1, 1))
    conv_rows = jnp.transpose(conv_t)
    gated = (gate_stream.astype(jnp.float32) * conv_rows).astype(jnp.bfloat16)
    partial_terms = jnp.dot(gated, out_weight, preferred_element_type=jnp.float32)
    return lax.psum_scatter(partial_terms, "chan", scatter_dimension=1, tiled=True).astype(
        jnp.bfloat16
    )


MESH = pl.DeviceIdType.MESH
LANES = 128
SUB = 8
WIDE = 256
CHUNKS = 32
FORWARDS = 8
SLABS = 4
PIECES = 2


def tree_sum(terms):
    while len(terms) > 1:
        pairs = [terms[i] + terms[i + 1] for i in range(0, len(terms) - 1, 2)]
        terms = pairs + terms[len(pairs) * 2 :]
    return terms[0]


def one_minus_exp(u):
    series = u * (1.0 - u / 2.0 * (1.0 - u / 3.0 * (1.0 - u / 4.0 * (1.0 - u / 5.0 * (1.0 - u / 6.0)))))
    return jnp.where(u > 0.25, 1.0 - jnp.exp(-u), series)


def kernel(
    stages,
    gate_hbm, key_hbm, value_hbm, res_hbm, decay_hbm, w_hbm, out,
    gate, key, value, res, decay, wbuf, sbuf, rbuf, gated,
    xs, ys, lam, base, dec, carried, ends, give, chip, peer_end, zbuf, give_state, peer_state, state,
    in_sem, w_sem, chunk_send, chunk_recv, pair_send, pair_recv, z_send, z_recv,
):
    rows = gate.shape[0]
    modes = res.shape[0]
    half_modes = modes // 2
    half_size = half_modes * SUB
    chan = lax.axis_index("chan")
    ctx = lax.axis_index("ctx")
    core = lax.rem(ctx, 2)
    stage = ctx // 2
    x = lax.rem(chan, 2)
    y = chan // 2
    along_x = y * 2 + (1 - x)
    along_y = (1 - y) * 2 + x
    across = (1 - y) * 2 + (1 - x)
    partner = stage * 2 + (1 - core)

    loads = [
        pltpu.make_async_copy(src, dst, in_sem.at[i])
        for i, (src, dst) in enumerate(
            [(decay_hbm, decay), (res_hbm, res), (gate_hbm, gate)]
        )
    ]
    slab = rows // SLABS

    def stream_load(i):
        src, dst = (key_hbm, key) if i % 2 == 0 else (value_hbm, value)
        here = pl.ds(i // 2 * slab, slab)
        return pltpu.make_async_copy(src.at[here, :], dst.at[here, :], in_sem.at[3 + i])

    for i in range(2 * SLABS):
        stream_load(i).start()
    for load in loads[:2]:
        load.start()

    def w_copy(i):
        owner = (across, along_y if i % 2 else along_x, along_x if i % 2 else along_y, chan)[i // 4]
        column = owner * (4 * WIDE) + (i % 2) * 2 * WIDE + (i // 2 % 2) * WIDE
        return pltpu.make_async_copy(
            w_hbm.at[:, pl.ds(pl.multiple_of(column, WIDE), WIDE)], wbuf.at[i], w_sem.at[i]
        )

    barrier = pltpu.get_barrier_semaphore()
    pl.semaphore_signal(barrier, inc=1, device_id=(along_x, ctx), device_id_type=MESH)
    pl.semaphore_signal(barrier, inc=1, device_id=(along_y, ctx), device_id_type=MESH)
    pl.semaphore_signal(barrier, inc=1, device_id=(chan, partner), device_id_type=MESH)
    for step in range(1, stages):
        other = lax.rem(stage + step, stages) * 2 + core
        pl.semaphore_signal(barrier, inc=1, device_id=(chan, other), device_id_type=MESH)

    loads[0].wait()
    loads[1].wait()
    for b in range(SUB):
        at = pl.ds(b, modes, stride=SUB)
        d = decay[:, b * LANES : (b + 1) * LANES]
        dec[at, :] = d
        lam[at, :] = jnp.exp(-d)
        base[at, :] = res[:, b * LANES : (b + 1) * LANES] * jnp.sqrt(one_minus_exp(2.0 * d))
    for part in range(SLABS):
        stream_load(2 * part).wait()
        stream_load(2 * part + 1).wait()
        here = slice(part * slab, (part + 1) * slab)
        for b in range(SUB):
            cols = slice(b * LANES, (b + 1) * LANES)
            mixed = key[here, cols].astype(jnp.float32) * value[here, cols].astype(jnp.float32)
            xs[pl.ds(part * slab * SUB + b, slab, stride=SUB), :] = mixed
    loads[2].start()
    for i in range(CHUNKS // 2):
        w_copy(i).start()

    def vec(t):
        return pl.ds(pl.multiple_of(t * SUB, SUB), SUB)

    def mode_rows(half, n):
        return pl.ds(pl.multiple_of(half * half_size + n * SUB, SUB), SUB)

    def half_rows(half):
        return pl.ds(pl.multiple_of(half * half_size, half_size), half_size)

    mid = rows // 2

    quarter = rows // 4
    piece_modes = half_modes // PIECES
    piece_size = piece_modes * SUB

    def end_states(half, piece, dst):
        numbers = range(piece * piece_modes, (piece + 1) * piece_modes)
        lams = [lam[mode_rows(half, n), :] for n in numbers]

        def step(t, carry):
            now = [xs[vec(t + q * quarter), :] for q in range(4)]
            return tuple(tuple(l * h + x for l, h in zip(lams, hidden)) for x, hidden in zip(now, carry))

        zero = tuple(jnp.zeros((SUB, LANES), jnp.float32) for _ in numbers)
        parts = lax.fori_loop(0, quarter, step, (zero,) * 4, unroll=4)
        for k, n in enumerate(numbers):
            shrink = jnp.exp(dec[mode_rows(half, n), :] * float(-quarter))
            total = parts[0][k]
            for q in range(1, 4):
                total = shrink * total + parts[q][k]
            dst[n * SUB : (n + 1) * SUB, :] = total

    def send_end(piece):
        here = pl.ds(piece * piece_size, piece_size)
        return pltpu.make_async_remote_copy(
            src_ref=give.at[here, :], dst_ref=peer_end.at[here, :],
            send_sem=pair_send.at[piece], recv_sem=pair_recv.at[piece],
            device_id=(chan, partner), device_id_type=MESH,
        )

    def push(step, piece):
        here = pl.ds(piece * piece_size, piece_size)
        sem = (step - 1) * PIECES + piece
        return pltpu.make_async_remote_copy(
            src_ref=chip.at[here, :], dst_ref=zbuf.at[step - 1, here, :],
            send_sem=z_send.at[sem], recv_sem=z_recv.at[sem],
            device_id=(chan, lax.rem(stage + step, stages) * 2 + core), device_id_type=MESH,
        )

    is_first = core == 0
    for piece in range(PIECES):
        end_states(1 - core, piece, give)
        if piece == 0:
            pl.semaphore_wait(barrier, 3 + stages - 1)
        send_end(piece).start()

    for piece in range(PIECES):
        end_states(core, piece, ends)
        send_end(piece).wait_recv()
        here = slice(piece * piece_size, (piece + 1) * piece_size)
        rates = dec[pl.ds(pl.multiple_of(core * half_size + piece * piece_size, piece_size), piece_size), :]
        own, peer = ends[here, :], peer_end[here, :]
        chip[here, :] = jnp.exp(rates * float(-rows)) * jnp.where(is_first, own, peer) + jnp.where(is_first, peer, own)
        for step in range(1, stages):
            @pl.when(stage + step < stages)
            def _():
                push(step, piece).start()

    def local_rows(part):
        lams = [lam[n * SUB : (n + 1) * SUB, :] for n in range(modes)]
        bases = [base[n * SUB : (n + 1) * SUB, :] for n in range(modes)]

        def step(t, hidden):
            now = xs[vec(t), :]
            hidden = tuple(l * h + now for l, h in zip(lams, hidden))
            ys[vec(t), :] = tree_sum([b * h for b, h in zip(bases, hidden)])
            return hidden

        if part:
            start = tuple(carried[n * SUB : (n + 1) * SUB, :] for n in range(modes))
        else:
            start = tuple(jnp.zeros((SUB, LANES), jnp.float32) for _ in range(modes))
        hidden = lax.fori_loop(part * mid, (part + 1) * mid, step, start, unroll=4)
        if not part:
            for n in range(modes):
                carried[n * SUB : (n + 1) * SUB, :] = hidden[n]

    local_rows(0)
    state[...] = jnp.zeros_like(state)
    for step in range(1, stages):
        @pl.when(stage >= step)
        def _():
            for piece in range(PIECES):
                push(step, piece).wait_recv()
            weight = jnp.exp(dec[half_rows(core), :] * float(-2 * rows * (step - 1)))
            state[...] += weight * zbuf[step - 1]

    span = jnp.exp(dec[half_rows(core), :] * float(-rows))
    end_first = jnp.where(is_first, ends[...], peer_end[...])
    begin_first = state[...]
    begin_second = span * begin_first + end_first
    give_state[...] = jnp.where(is_first, begin_second, begin_first)
    send_state = pltpu.make_async_remote_copy(
        src_ref=give_state, dst_ref=peer_state, send_sem=pair_send.at[PIECES], recv_sem=pair_recv.at[PIECES],
        device_id=(chan, partner), device_id_type=MESH,
    )
    send_state.start()
    state[...] = jnp.where(is_first, begin_first, begin_second)

    def add_state(half, src, part):
        lams = [lam[mode_rows(half, n), :] for n in range(half_modes)]
        start = part * mid
        low, high = [], []
        for n in range(half_modes):
            d = dec[mode_rows(half, n), :]
            first = base[mode_rows(half, n), :] * src[n * SUB : (n + 1) * SUB, :]
            low.append(first * jnp.exp(d * float(-start)) if part else first)
            high.append(first * jnp.exp(d * float(-start - quarter)))

        def step(t, carry):
            low, high = carry
            low = tuple(l * h for l, h in zip(lams, low))
            high = tuple(l * h for l, h in zip(lams, high))
            ys[vec(t + start), :] += tree_sum(list(low))
            ys[vec(t + start + quarter), :] += tree_sum(list(high))
            return (low, high)

        lax.fori_loop(0, quarter, step, (tuple(low), tuple(high)), unroll=4)

    def gate_rows(part):
        here = slice(part * mid, (part + 1) * mid)
        for b in range(SUB):
            cols = slice(b * LANES, (b + 1) * LANES)
            conv = ys[pl.ds(part * mid * SUB + b, mid, stride=SUB), :]
            gated[here, cols] = (gate[here, cols].astype(jnp.float32) * conv).astype(jnp.bfloat16)

    def chunk_copy(i, target):
        return pltpu.make_async_remote_copy(
            src_ref=sbuf.at[i], dst_ref=rbuf.at[i], send_sem=chunk_send.at[i], recv_sem=chunk_recv.at[i],
            device_id=(target, ctx), device_id_type=MESH,
        )

    def first_target(i):
        odd = lax.rem(i, 2)
        return along_x * (1 - odd) + along_y * odd

    def second_target(i):
        odd = lax.rem(i, 2)
        return along_y * (1 - odd) + along_x * odd

    def w_wait(i):
        pltpu.make_async_copy(w_hbm.at[:, pl.ds(0, WIDE)], wbuf.at[i], w_sem.at[i]).wait()

    def block_of(i):
        return i // 8 * 4 + lax.rem(i, 4)

    def partial_sum(i):
        part = lax.rem(i // 4, 2)
        here = pl.ds(pl.multiple_of(part * mid, mid), mid)
        sbuf[i] = jnp.dot(gated[here, :], wbuf[block_of(i)], preferred_element_type=jnp.float32)

    add_state(core, state, 0)
    send_state.wait_recv()
    add_state(1 - core, peer_state, 0)
    loads[2].wait()
    gate_rows(0)

    @pl.loop(0, 4)
    def _(i):
        w_wait(i)
        partial_sum(i)
        chunk_copy(i, first_target(i)).start()

    local_rows(1)
    add_state(core, state, 1)
    add_state(1 - core, peer_state, 1)
    gate_rows(1)

    @pl.loop(4, CHUNKS)
    def _(i):
        @pl.when(lax.rem(i // 4, 2) == 0)
        def _():
            w_wait(block_of(i))

        partial_sum(i)

        @pl.when(i < FORWARDS)
        def _():
            chunk_copy(i, first_target(i)).start()

    @pl.loop(0, FORWARDS)
    def _(j):
        chunk_copy(j, first_target(j)).wait_send()
        chunk_copy(j + FORWARDS, first_target(j)).start()

    @pl.loop(0, FORWARDS)
    def _(j):
        chunk_copy(j, first_target(j)).wait_recv()
        sbuf[j + 2 * FORWARDS] += rbuf[j]
        chunk_copy(j + 2 * FORWARDS, second_target(j)).start()

    @pl.loop(0, FORWARDS)
    def _(j):
        chunk_copy(j + FORWARDS, first_target(j)).wait_recv()
        sbuf[j + 3 * FORWARDS] += rbuf[j + FORWARDS]

    @pl.loop(0, FORWARDS)
    def _(j):
        chunk_copy(j + 2 * FORWARDS, second_target(j)).wait_recv()
        here = pl.ds(pl.multiple_of(j // 4 * mid, mid), mid)
        column = lax.rem(j, 2) * (2 * WIDE) + lax.rem(j // 2, 2) * WIDE
        cols = pl.ds(pl.multiple_of(column, WIDE), WIDE)
        out[here, cols] = (sbuf[j + 3 * FORWARDS] + rbuf[j + 2 * FORWARDS]).astype(jnp.bfloat16)

    for piece in range(PIECES):
        send_end(piece).wait_send()
    send_state.wait_send()
    for step in range(1, stages):
        @pl.when(stage + step < stages)
        def _():
            for piece in range(PIECES):
                push(step, piece).wait_send()

    @pl.loop(0, FORWARDS)
    def _(j):
        chunk_copy(j + FORWARDS, first_target(j)).wait_send()
        chunk_copy(j + 2 * FORWARDS, second_target(j)).wait_send()


def fused(gate_stream, key_stream, value_stream, residues, decay_rates, out_weight):
    rows, channels = gate_stream.shape
    modes = residues.shape[0]
    stages = lax.axis_size("ctx") // 2
    f32, bf16 = jnp.float32, jnp.bfloat16
    whole = (modes * SUB, LANES)
    half = (modes // 2 * SUB, LANES)
    dma = pltpu.SemaphoreType.DMA
    return pl.pallas_call(
        functools.partial(kernel, stages),
        out_shape=pltpu.VMEM((rows, 4 * WIDE), bf16),
        in_specs=[pl.BlockSpec(memory_space=pltpu.HBM)] * 6,
        out_specs=pl.BlockSpec(memory_space=pltpu.VMEM),
        scratch_shapes=[
            pltpu.VMEM((rows, channels), bf16),
            pltpu.VMEM((rows, channels), bf16),
            pltpu.VMEM((rows, channels), bf16),
            pltpu.VMEM((modes, channels), f32),
            pltpu.VMEM((modes, channels), f32),
            pltpu.VMEM((CHUNKS // 2, channels, WIDE), bf16),
            pltpu.VMEM((CHUNKS, rows // 2, WIDE), f32),
            pltpu.VMEM((3 * FORWARDS, rows // 2, WIDE), f32),
            pltpu.VMEM((rows, channels), bf16),
            pltpu.VMEM((rows * SUB, LANES), f32),
            pltpu.VMEM((rows * SUB, LANES), f32),
            pltpu.VMEM(whole, f32),
            pltpu.VMEM(whole, f32),
            pltpu.VMEM(whole, f32),
            pltpu.VMEM(whole, f32),
            pltpu.VMEM(half, f32),
            pltpu.VMEM(half, f32),
            pltpu.VMEM(half, f32),
            pltpu.VMEM(half, f32),
            pltpu.VMEM((stages - 1,) + half, f32),
            pltpu.VMEM(half, f32),
            pltpu.VMEM(half, f32),
            pltpu.VMEM(half, f32),
            dma((3 + 2 * SLABS,)),
            dma((CHUNKS // 2,)),
            dma((3 * FORWARDS,)),
            dma((3 * FORWARDS,)),
            dma((PIECES + 1,)),
            dma((PIECES + 1,)),
            dma((PIECES * (stages - 1),)),
            dma((PIECES * (stages - 1),)),
        ],
        compiler_params=pltpu.CompilerParams(
            collective_id=0, has_side_effects=True, vmem_limit_bytes=63 * 1024 * 1024
        ),
        cost_estimate=pl.CostEstimate(
            flops=2 * rows * channels * 16 * WIDE, bytes_accessed=2 * channels * 16 * WIDE, transcendentals=0
        ),
    )(gate_stream, key_stream, value_stream, residues, decay_rates, out_weight)


def run(*arrays):
    square = lax.axis_size("chan") == 4 and lax.axis_size("ctx") % 2 == 0 and lax.axis_size("ctx") > 2
    fits = arrays[0].shape[1] == SUB * LANES and arrays[5].shape[1] == 16 * WIDE
    return (fused if square and fits else on_device)(*arrays)


def solution(mesh):
    return jax.shard_map(
        run,
        mesh=mesh,
        in_specs=(
            P("ctx", "chan"),
            P("ctx", "chan"),
            P("ctx", "chan"),
            P(None, "chan"),
            P(None, "chan"),
            P("chan", None),
        ),
        out_specs=P("ctx", "chan"),
        check_vma=False,
    )
```

```python
import functools
import math

import jax
import jax.numpy as jnp
from jax import lax
from jax.experimental import pallas as pl
from jax.experimental.pallas import tpu as pltpu
from jax.sharding import PartitionSpec as P

HIGH = lax.Precision.HIGHEST
TWO_PI = 2.0 * math.pi


def swapped(block, axis, distance):
    count = lax.axis_size(axis)
    route = []
    for low in range(count):
        high = low | 1 << distance
        if high != low and high < count:
            route += [(low, high), (high, low)]
    return lax.ppermute(block, axis, route)


def unit_circle(numer, denom):
    angle = TWO_PI * numer.astype(jnp.float32) / denom
    return (jnp.cos(angle), jnp.sin(angle))


def times(ar, ai, br, bi):
    return (ar * br - ai * bi, ar * bi + ai * br)


def dft_matrix(length, inverse):
    index = jnp.arange(length, dtype=jnp.int32)
    cosine, sine = unit_circle(index[:, None] * index[None, :] % length, length)
    if inverse:
        top = jnp.concatenate([cosine, sine], axis=1)
        bottom = jnp.concatenate([-sine, cosine], axis=1)
    else:
        top = jnp.concatenate([cosine, -sine], axis=1)
        bottom = jnp.concatenate([sine, cosine], axis=1)
    return jnp.concatenate([top, bottom], axis=0)


def along_time(real_part, imag_part, matrix):
    rows = real_part.shape[-1]
    stacked = jnp.concatenate([real_part, imag_part], axis=-1)
    result = jnp.dot(stacked, matrix, precision=HIGH)
    return (result[..., :rows], result[..., rows:])


def filter_terms(residues, decay_rates, length):
    lam = jnp.exp(-decay_rates)
    one_less = -jnp.expm1(-decay_rates)
    base = residues * jnp.sqrt(-jnp.expm1(-2.0 * decay_rates))
    tail = jnp.exp(-decay_rates * length)
    return (base, lam, one_less, tail)


def response(freq, total, filt):
    base, lam, one_less, tail = filt
    wrapped = freq % total
    cosine, sine = unit_circle(wrapped, total)
    half_sine = jnp.sin(math.pi * wrapped.astype(jnp.float32) / total)
    parity_sign = 1.0 - 2.0 * (wrapped % 2).astype(jnp.float32)
    resp_r = 0.0
    resp_i = 0.0
    for mode in range(base.shape[0]):
        numer = base[mode] * (1.0 - tail[mode] * parity_sign)
        den_r = one_less[mode] + 2.0 * lam[mode] * half_sine * half_sine
        den_i = lam[mode] * sine
        norm_sq = den_r * den_r + den_i * den_i
        resp_r = resp_r + numer * den_r / norm_sq
        resp_i = resp_i - numer * den_i / norm_sq
    return (resp_r, resp_i)


def spectral(spec_r, spec_i, q_index, filt, big_p, rows):
    total = 2 * big_p * rows
    fsel = jnp.arange(2, dtype=jnp.int32).reshape((2,) + (1,) * (spec_r.ndim - 1))
    freq = 2 * q_index + fsel
    pos = jnp.arange(rows, dtype=jnp.int32)
    cosine, sine = unit_circle(pos * freq % total, total)
    tw_r, tw_i = times(spec_r, spec_i, cosine, -sine)
    full_r, full_i = along_time(tw_r, tw_i, dft_matrix(rows, False))
    resp_r, resp_i = response(freq + 2 * big_p * pos, total, filt)
    prod_r, prod_i = times(full_r, full_i, resp_r, resp_i)
    back_r, back_i = along_time(prod_r, prod_i, dft_matrix(rows, True))
    return times(back_r, back_i, cosine, sine)


def pre_twiddle(mixed, p_index, big_p, shape_f):
    fsel = jnp.arange(2, dtype=jnp.int32).reshape(shape_f)
    cosine, sine = unit_circle(p_index * fsel % (2 * big_p), 2 * big_p)
    return (mixed * cosine, -mixed * sine)


def post_twiddle(spec_r, spec_i, p_index, big_p, rows, shape_f):
    fsel = jnp.arange(2, dtype=jnp.int32).reshape(shape_f)
    cosine, sine = unit_circle(p_index * fsel % (2 * big_p), 2 * big_p)
    return jnp.sum(cosine * spec_r - sine * spec_i, axis=0) / (2.0 * big_p * rows)


def reverse_bits(device, bits):
    result = jnp.zeros_like(device)
    for bit in range(bits):
        result = result | (device >> bit & 1) << bits - 1 - bit
    return result


def butterfly_forward(real_part, imag_part, device, bits):
    for bit in range(bits - 1, -1, -1):
        half = 1 << bit
        place = device % (2 * half)
        upper = place >= half
        other_r, other_i = swapped((real_part, imag_part), "ctx", bit)
        cosine, sine = unit_circle(jnp.where(upper, place - half, 0), 2 * half)
        tw_r, tw_i = times(other_r - real_part, other_i - imag_part, cosine, -sine)
        real_part = jnp.where(upper, tw_r, real_part + other_r)
        imag_part = jnp.where(upper, tw_i, imag_part + other_i)
    return (real_part, imag_part)


def butterfly_inverse(real_part, imag_part, device, bits):
    for bit in range(bits):
        half = 1 << bit
        place = device % (2 * half)
        upper = place >= half
        cosine, sine = unit_circle(jnp.where(upper, place - half, 0), 2 * half)
        tw_r, tw_i = times(real_part, imag_part, cosine, sine)
        send_r = jnp.where(upper, tw_r, real_part)
        send_i = jnp.where(upper, tw_i, imag_part)
        other_r, other_i = swapped((send_r, send_i), "ctx", bit)
        real_part = jnp.where(upper, other_r - tw_r, real_part + other_r)
        imag_part = jnp.where(upper, other_i - tw_i, imag_part + other_i)
    return (real_part, imag_part)


def on_device(gate_stream, key_stream, value_stream, residues, decay_rates, out_weight):
    big_p = lax.axis_size("ctx")
    bits = big_p.bit_length() - 1
    rows = key_stream.shape[0]
    length = float(big_p * rows)
    device = lax.axis_index("ctx")
    mixed = jnp.transpose(key_stream.astype(jnp.float32) * value_stream.astype(jnp.float32))
    base, lam, one_less, tail = filter_terms(residues, decay_rates, length)
    filt = (base[:, :, None], lam[:, :, None], one_less[:, :, None], tail[:, :, None])
    z_r, z_i = pre_twiddle(mixed, device, big_p, (2, 1, 1))
    y_r, y_i = butterfly_forward(z_r, z_i, device, bits)
    q_index = reverse_bits(device, bits)
    u_r, u_i = spectral(y_r, y_i, q_index, filt, big_p, rows)
    v_r, v_i = butterfly_inverse(u_r, u_i, device, bits)
    conv_t = post_twiddle(v_r, v_i, device, big_p, rows, (2, 1, 1))
    conv_rows = jnp.transpose(conv_t)
    gated = (gate_stream.astype(jnp.float32) * conv_rows).astype(jnp.bfloat16)
    partial_terms = jnp.dot(gated, out_weight, preferred_element_type=jnp.float32)
    return lax.psum_scatter(partial_terms, "chan", scatter_dimension=1, tiled=True).astype(
        jnp.bfloat16
    )


MESH = pl.DeviceIdType.MESH
LANES = 128
SUB = 8
WIDE = 512
CHUNKS = 16
FORWARDS = 4
SLABS = 4


def tree_sum(terms):
    while len(terms) > 1:
        pairs = [terms[i] + terms[i + 1] for i in range(0, len(terms) - 1, 2)]
        terms = pairs + terms[len(pairs) * 2 :]
    return terms[0]


def one_minus_exp(u):
    series = u * (1.0 - u / 2.0 * (1.0 - u / 3.0 * (1.0 - u / 4.0 * (1.0 - u / 5.0 * (1.0 - u / 6.0)))))
    return jnp.where(u > 0.25, 1.0 - jnp.exp(-u), series)


def kernel(
    stages,
    gate_hbm, key_hbm, value_hbm, res_hbm, decay_hbm, w_hbm, out,
    gate, key, value, res, decay, wbuf, sbuf, rbuf, gated,
    xs, ys, lam, base, dec, carried, ends, give, chip, peer_end, zbuf, give_state, peer_state, state,
    in_sem, w_sem, chunk_send, chunk_recv, pair_send, pair_recv, z_send, z_recv,
):
    rows = gate.shape[0]
    modes = res.shape[0]
    half_modes = modes // 2
    half_size = half_modes * SUB
    chan = lax.axis_index("chan")
    ctx = lax.axis_index("ctx")
    core = lax.rem(ctx, 2)
    stage = ctx // 2
    x = lax.rem(chan, 2)
    y = chan // 2
    along_x = y * 2 + (1 - x)
    along_y = (1 - y) * 2 + x
    across = (1 - y) * 2 + (1 - x)
    partner = stage * 2 + (1 - core)

    loads = [
        pltpu.make_async_copy(src, dst, in_sem.at[i])
        for i, (src, dst) in enumerate(
            [(decay_hbm, decay), (res_hbm, res), (gate_hbm, gate)]
        )
    ]
    slab = rows // SLABS

    def stream_load(i):
        src, dst = (key_hbm, key) if i % 2 == 0 else (value_hbm, value)
        here = pl.ds(i // 2 * slab, slab)
        return pltpu.make_async_copy(src.at[here, :], dst.at[here, :], in_sem.at[3 + i])

    for i in range(2 * SLABS):
        stream_load(i).start()
    for load in loads[:2]:
        load.start()

    def w_copy(i):
        owner = (across, along_y if i % 2 else along_x, along_x if i % 2 else along_y, chan)[i // 2]
        column = owner * (2 * WIDE) + (i % 2) * WIDE
        return pltpu.make_async_copy(
            w_hbm.at[:, pl.ds(pl.multiple_of(column, WIDE), WIDE)], wbuf.at[i], w_sem.at[i]
        )

    barrier = pltpu.get_barrier_semaphore()
    pl.semaphore_signal(barrier, inc=1, device_id=(along_x, ctx), device_id_type=MESH)
    pl.semaphore_signal(barrier, inc=1, device_id=(along_y, ctx), device_id_type=MESH)
    pl.semaphore_signal(barrier, inc=1, device_id=(chan, partner), device_id_type=MESH)
    for step in range(1, stages):
        other = lax.rem(stage + step, stages) * 2 + core
        pl.semaphore_signal(barrier, inc=1, device_id=(chan, other), device_id_type=MESH)

    loads[0].wait()
    loads[1].wait()
    for b in range(SUB):
        at = pl.ds(b, modes, stride=SUB)
        d = decay[:, b * LANES : (b + 1) * LANES]
        dec[at, :] = d
        lam[at, :] = jnp.exp(-d)
        base[at, :] = res[:, b * LANES : (b + 1) * LANES] * jnp.sqrt(one_minus_exp(2.0 * d))
    for part in range(SLABS):
        stream_load(2 * part).wait()
        stream_load(2 * part + 1).wait()
        here = slice(part * slab, (part + 1) * slab)
        for b in range(SUB):
            cols = slice(b * LANES, (b + 1) * LANES)
            mixed = key[here, cols].astype(jnp.float32) * value[here, cols].astype(jnp.float32)
            xs[pl.ds(part * slab * SUB + b, slab, stride=SUB), :] = mixed
    loads[2].start()
    for i in range(CHUNKS // 2):
        w_copy(i).start()

    def vec(t):
        return pl.ds(pl.multiple_of(t * SUB, SUB), SUB)

    def mode_rows(half, n):
        return pl.ds(pl.multiple_of(half * half_size + n * SUB, SUB), SUB)

    def half_rows(half):
        return pl.ds(pl.multiple_of(half * half_size, half_size), half_size)

    mid = rows // 2

    def end_states(half, dst):
        lams = [lam[mode_rows(half, n), :] for n in range(half_modes)]

        def step(t, carry):
            low, high = carry
            x_low = xs[vec(t), :]
            x_high = xs[vec(t + mid), :]
            low = tuple(l * h + x_low for l, h in zip(lams, low))
            high = tuple(l * h + x_high for l, h in zip(lams, high))
            return (low, high)

        zero = tuple(jnp.zeros((SUB, LANES), jnp.float32) for _ in range(half_modes))
        low, high = lax.fori_loop(0, mid, step, (zero, zero), unroll=4)
        for n in range(half_modes):
            shrink = jnp.exp(dec[mode_rows(half, n), :] * float(-mid))
            dst[n * SUB : (n + 1) * SUB, :] = shrink * low[n] + high[n]

    end_states(1 - core, give)
    pl.semaphore_wait(barrier, 3 + stages - 1)
    send_end = pltpu.make_async_remote_copy(
        src_ref=give, dst_ref=peer_end, send_sem=pair_send.at[0], recv_sem=pair_recv.at[0],
        device_id=(chan, partner), device_id_type=MESH,
    )
    send_end.start()
    end_states(core, ends)
    send_end.wait_recv()

    own_decay = dec[half_rows(core), :]
    span = jnp.exp(own_decay * float(-rows))
    is_first = core == 0
    end_first = jnp.where(is_first, ends[...], peer_end[...])
    end_second = jnp.where(is_first, peer_end[...], ends[...])
    chip[...] = span * end_first + end_second

    def push(step):
        return pltpu.make_async_remote_copy(
            src_ref=chip, dst_ref=zbuf.at[step - 1], send_sem=z_send.at[step - 1], recv_sem=z_recv.at[step - 1],
            device_id=(chan, lax.rem(stage + step, stages) * 2 + core), device_id_type=MESH,
        )

    for step in range(1, stages):
        @pl.when(stage + step < stages)
        def _():
            push(step).start()

    def local_rows(part):
        lams = [lam[n * SUB : (n + 1) * SUB, :] for n in range(modes)]
        bases = [base[n * SUB : (n + 1) * SUB, :] for n in range(modes)]

        def step(t, hidden):
            now = xs[vec(t), :]
            hidden = tuple(l * h + now for l, h in zip(lams, hidden))
            ys[vec(t), :] = tree_sum([b * h for b, h in zip(bases, hidden)])
            return hidden

        if part:
            start = tuple(carried[n * SUB : (n + 1) * SUB, :] for n in range(modes))
        else:
            start = tuple(jnp.zeros((SUB, LANES), jnp.float32) for _ in range(modes))
        hidden = lax.fori_loop(part * mid, (part + 1) * mid, step, start, unroll=4)
        if not part:
            for n in range(modes):
                carried[n * SUB : (n + 1) * SUB, :] = hidden[n]

    local_rows(0)
    state[...] = jnp.zeros_like(state)
    for step in range(1, stages):
        @pl.when(stage >= step)
        def _():
            push(step).wait_recv()
            weight = jnp.exp(dec[half_rows(core), :] * float(-2 * rows * (step - 1)))
            state[...] += weight * zbuf[step - 1]

    begin_first = state[...]
    begin_second = span * begin_first + end_first
    give_state[...] = jnp.where(is_first, begin_second, begin_first)
    send_state = pltpu.make_async_remote_copy(
        src_ref=give_state, dst_ref=peer_state, send_sem=pair_send.at[1], recv_sem=pair_recv.at[1],
        device_id=(chan, partner), device_id_type=MESH,
    )
    send_state.start()
    state[...] = jnp.where(is_first, begin_first, begin_second)

    quarter = rows // 4

    def add_state(half, src, part):
        lams = [lam[mode_rows(half, n), :] for n in range(half_modes)]
        start = part * mid
        low, high = [], []
        for n in range(half_modes):
            d = dec[mode_rows(half, n), :]
            first = base[mode_rows(half, n), :] * src[n * SUB : (n + 1) * SUB, :]
            low.append(first * jnp.exp(d * float(-start)) if part else first)
            high.append(first * jnp.exp(d * float(-start - quarter)))

        def step(t, carry):
            low, high = carry
            low = tuple(l * h for l, h in zip(lams, low))
            high = tuple(l * h for l, h in zip(lams, high))
            ys[vec(t + start), :] += tree_sum(list(low))
            ys[vec(t + start + quarter), :] += tree_sum(list(high))
            return (low, high)

        lax.fori_loop(0, quarter, step, (tuple(low), tuple(high)), unroll=4)

    def gate_rows(part):
        here = slice(part * mid, (part + 1) * mid)
        for b in range(SUB):
            cols = slice(b * LANES, (b + 1) * LANES)
            conv = ys[pl.ds(part * mid * SUB + b, mid, stride=SUB), :]
            gated[here, cols] = (gate[here, cols].astype(jnp.float32) * conv).astype(jnp.bfloat16)

    def chunk_copy(i, target):
        return pltpu.make_async_remote_copy(
            src_ref=sbuf.at[i], dst_ref=rbuf.at[i], send_sem=chunk_send.at[i], recv_sem=chunk_recv.at[i],
            device_id=(target, ctx), device_id_type=MESH,
        )

    def first_target(i):
        odd = lax.rem(i, 2)
        return along_x * (1 - odd) + along_y * odd

    def second_target(i):
        odd = lax.rem(i, 2)
        return along_y * (1 - odd) + along_x * odd

    def w_wait(i):
        pltpu.make_async_copy(w_hbm.at[:, pl.ds(0, WIDE)], wbuf.at[i], w_sem.at[i]).wait()

    def block_of(i):
        return i // 4 * 2 + lax.rem(i, 2)

    def slot_of(i):
        paired = i // 4 * 4 + lax.rem(i, 2) * 2 + lax.rem(i // 2, 2)
        return jnp.where(i // 4 == 1, paired, i)

    def direct_copy(parity):
        both = pl.ds(FORWARDS + 2 * parity, 2)
        return pltpu.make_async_remote_copy(
            src_ref=sbuf.at[both], dst_ref=rbuf.at[both],
            send_sem=chunk_send.at[FORWARDS + parity], recv_sem=chunk_recv.at[FORWARDS + parity],
            device_id=(first_target(parity), ctx), device_id_type=MESH,
        )

    def partial_sum(i):
        part = lax.rem(i // 2, 2)
        here = pl.ds(pl.multiple_of(part * mid, mid), mid)
        sbuf[slot_of(i)] = jnp.dot(gated[here, :], wbuf[block_of(i)], preferred_element_type=jnp.float32)

    add_state(core, state, 0)
    send_state.wait_recv()
    add_state(1 - core, peer_state, 0)
    loads[2].wait()
    gate_rows(0)

    @pl.loop(0, 2)
    def _(i):
        w_wait(i)
        partial_sum(i)
        chunk_copy(i, first_target(i)).start()

    local_rows(1)
    add_state(core, state, 1)
    add_state(1 - core, peer_state, 1)
    gate_rows(1)

    @pl.loop(2, CHUNKS)
    def _(i):
        @pl.when(lax.rem(i // 2, 2) == 0)
        def _():
            w_wait(block_of(i))

        partial_sum(i)

        @pl.when(i < FORWARDS)
        def _():
            chunk_copy(i, first_target(i)).start()

        @pl.when(i // 2 == 3)
        def _():
            direct_copy(lax.rem(i, 2)).start()

    @pl.loop(0, FORWARDS)
    def _(j):
        chunk_copy(j, first_target(j)).wait_recv()
        sbuf[j + 2 * FORWARDS] += rbuf[j]
        chunk_copy(j + 2 * FORWARDS, second_target(j)).start()

    @pl.loop(0, 2)
    def _(parity):
        direct_copy(parity).wait_recv()
        for k in range(2):
            sbuf[3 * FORWARDS + 2 * k + parity] += rbuf[FORWARDS + 2 * parity + k]

    @pl.loop(0, FORWARDS)
    def _(j):
        chunk_copy(j + 2 * FORWARDS, second_target(j)).wait_recv()
        here = pl.ds(pl.multiple_of(j // 2 * mid, mid), mid)
        cols = pl.ds(pl.multiple_of(lax.rem(j, 2) * WIDE, WIDE), WIDE)
        out[here, cols] = (sbuf[j + 3 * FORWARDS] + rbuf[j + 2 * FORWARDS]).astype(jnp.bfloat16)

    send_end.wait_send()
    send_state.wait_send()
    for parity in range(2):
        direct_copy(parity).wait_send()
    for step in range(1, stages):
        @pl.when(stage + step < stages)
        def _():
            push(step).wait_send()

    @pl.loop(0, FORWARDS)
    def _(j):
        chunk_copy(j, first_target(j)).wait_send()
        chunk_copy(j + 2 * FORWARDS, second_target(j)).wait_send()


def fused(gate_stream, key_stream, value_stream, residues, decay_rates, out_weight):
    rows, channels = gate_stream.shape
    modes = residues.shape[0]
    stages = lax.axis_size("ctx") // 2
    f32, bf16 = jnp.float32, jnp.bfloat16
    whole = (modes * SUB, LANES)
    half = (modes // 2 * SUB, LANES)
    dma = pltpu.SemaphoreType.DMA
    return pl.pallas_call(
        functools.partial(kernel, stages),
        out_shape=pltpu.VMEM((rows, 2 * WIDE), bf16),
        in_specs=[pl.BlockSpec(memory_space=pltpu.HBM)] * 6,
        out_specs=pl.BlockSpec(memory_space=pltpu.VMEM),
        scratch_shapes=[
            pltpu.VMEM((rows, channels), bf16),
            pltpu.VMEM((rows, channels), bf16),
            pltpu.VMEM((rows, channels), bf16),
            pltpu.VMEM((modes, channels), f32),
            pltpu.VMEM((modes, channels), f32),
            pltpu.VMEM((CHUNKS // 2, channels, WIDE), bf16),
            pltpu.VMEM((CHUNKS, rows // 2, WIDE), f32),
            pltpu.VMEM((3 * FORWARDS, rows // 2, WIDE), f32),
            pltpu.VMEM((rows, channels), bf16),
            pltpu.VMEM((rows * SUB, LANES), f32),
            pltpu.VMEM((rows * SUB, LANES), f32),
            pltpu.VMEM(whole, f32),
            pltpu.VMEM(whole, f32),
            pltpu.VMEM(whole, f32),
            pltpu.VMEM(whole, f32),
            pltpu.VMEM(half, f32),
            pltpu.VMEM(half, f32),
            pltpu.VMEM(half, f32),
            pltpu.VMEM(half, f32),
            pltpu.VMEM((stages - 1,) + half, f32),
            pltpu.VMEM(half, f32),
            pltpu.VMEM(half, f32),
            pltpu.VMEM(half, f32),
            dma((3 + 2 * SLABS,)),
            dma((CHUNKS // 2,)),
            dma((3 * FORWARDS,)),
            dma((3 * FORWARDS,)),
            dma((2,)),
            dma((2,)),
            dma((stages - 1,)),
            dma((stages - 1,)),
        ],
        compiler_params=pltpu.CompilerParams(
            collective_id=0, has_side_effects=True, vmem_limit_bytes=63 * 1024 * 1024
        ),
        cost_estimate=pl.CostEstimate(
            flops=2 * rows * channels * 8 * WIDE, bytes_accessed=2 * channels * 8 * WIDE, transcendentals=0
        ),
    )(gate_stream, key_stream, value_stream, residues, decay_rates, out_weight)


def run(*arrays):
    square = lax.axis_size("chan") == 4 and lax.axis_size("ctx") % 2 == 0 and lax.axis_size("ctx") > 2
    fits = arrays[0].shape[1] == SUB * LANES and arrays[5].shape[1] == 8 * WIDE
    return (fused if square and fits else on_device)(*arrays)


def solution(mesh):
    return jax.shard_map(
        run,
        mesh=mesh,
        in_specs=(
            P("ctx", "chan"),
            P("ctx", "chan"),
            P("ctx", "chan"),
            P(None, "chan"),
            P(None, "chan"),
            P("chan", None),
        ),
        out_specs=P("ctx", "chan"),
        check_vma=False,
    )
```

```python
import functools
import math

import jax
import jax.numpy as jnp
from jax import lax
from jax.experimental import pallas as pl
from jax.experimental.pallas import tpu as pltpu
from jax.sharding import PartitionSpec as P

HIGH = lax.Precision.HIGHEST
TWO_PI = 2.0 * math.pi


def swapped(block, axis, distance):
    count = lax.axis_size(axis)
    route = []
    for low in range(count):
        high = low | 1 << distance
        if high != low and high < count:
            route += [(low, high), (high, low)]
    return lax.ppermute(block, axis, route)


def unit_circle(numer, denom):
    angle = TWO_PI * numer.astype(jnp.float32) / denom
    return (jnp.cos(angle), jnp.sin(angle))


def times(ar, ai, br, bi):
    return (ar * br - ai * bi, ar * bi + ai * br)


def dft_matrix(length, inverse):
    index = jnp.arange(length, dtype=jnp.int32)
    cosine, sine = unit_circle(index[:, None] * index[None, :] % length, length)
    if inverse:
        top = jnp.concatenate([cosine, sine], axis=1)
        bottom = jnp.concatenate([-sine, cosine], axis=1)
    else:
        top = jnp.concatenate([cosine, -sine], axis=1)
        bottom = jnp.concatenate([sine, cosine], axis=1)
    return jnp.concatenate([top, bottom], axis=0)


def along_time(real_part, imag_part, matrix):
    rows = real_part.shape[-1]
    stacked = jnp.concatenate([real_part, imag_part], axis=-1)
    result = jnp.dot(stacked, matrix, precision=HIGH)
    return (result[..., :rows], result[..., rows:])


def filter_terms(residues, decay_rates, length):
    lam = jnp.exp(-decay_rates)
    one_less = -jnp.expm1(-decay_rates)
    base = residues * jnp.sqrt(-jnp.expm1(-2.0 * decay_rates))
    tail = jnp.exp(-decay_rates * length)
    return (base, lam, one_less, tail)


def response(freq, total, filt):
    base, lam, one_less, tail = filt
    wrapped = freq % total
    cosine, sine = unit_circle(wrapped, total)
    half_sine = jnp.sin(math.pi * wrapped.astype(jnp.float32) / total)
    parity_sign = 1.0 - 2.0 * (wrapped % 2).astype(jnp.float32)
    resp_r = 0.0
    resp_i = 0.0
    for mode in range(base.shape[0]):
        numer = base[mode] * (1.0 - tail[mode] * parity_sign)
        den_r = one_less[mode] + 2.0 * lam[mode] * half_sine * half_sine
        den_i = lam[mode] * sine
        norm_sq = den_r * den_r + den_i * den_i
        resp_r = resp_r + numer * den_r / norm_sq
        resp_i = resp_i - numer * den_i / norm_sq
    return (resp_r, resp_i)


def spectral(spec_r, spec_i, q_index, filt, big_p, rows):
    total = 2 * big_p * rows
    fsel = jnp.arange(2, dtype=jnp.int32).reshape((2,) + (1,) * (spec_r.ndim - 1))
    freq = 2 * q_index + fsel
    pos = jnp.arange(rows, dtype=jnp.int32)
    cosine, sine = unit_circle(pos * freq % total, total)
    tw_r, tw_i = times(spec_r, spec_i, cosine, -sine)
    full_r, full_i = along_time(tw_r, tw_i, dft_matrix(rows, False))
    resp_r, resp_i = response(freq + 2 * big_p * pos, total, filt)
    prod_r, prod_i = times(full_r, full_i, resp_r, resp_i)
    back_r, back_i = along_time(prod_r, prod_i, dft_matrix(rows, True))
    return times(back_r, back_i, cosine, sine)


def pre_twiddle(mixed, p_index, big_p, shape_f):
    fsel = jnp.arange(2, dtype=jnp.int32).reshape(shape_f)
    cosine, sine = unit_circle(p_index * fsel % (2 * big_p), 2 * big_p)
    return (mixed * cosine, -mixed * sine)


def post_twiddle(spec_r, spec_i, p_index, big_p, rows, shape_f):
    fsel = jnp.arange(2, dtype=jnp.int32).reshape(shape_f)
    cosine, sine = unit_circle(p_index * fsel % (2 * big_p), 2 * big_p)
    return jnp.sum(cosine * spec_r - sine * spec_i, axis=0) / (2.0 * big_p * rows)


def reverse_bits(device, bits):
    result = jnp.zeros_like(device)
    for bit in range(bits):
        result = result | (device >> bit & 1) << bits - 1 - bit
    return result


def butterfly_forward(real_part, imag_part, device, bits):
    for bit in range(bits - 1, -1, -1):
        half = 1 << bit
        place = device % (2 * half)
        upper = place >= half
        other_r, other_i = swapped((real_part, imag_part), "ctx", bit)
        cosine, sine = unit_circle(jnp.where(upper, place - half, 0), 2 * half)
        tw_r, tw_i = times(other_r - real_part, other_i - imag_part, cosine, -sine)
        real_part = jnp.where(upper, tw_r, real_part + other_r)
        imag_part = jnp.where(upper, tw_i, imag_part + other_i)
    return (real_part, imag_part)


def butterfly_inverse(real_part, imag_part, device, bits):
    for bit in range(bits):
        half = 1 << bit
        place = device % (2 * half)
        upper = place >= half
        cosine, sine = unit_circle(jnp.where(upper, place - half, 0), 2 * half)
        tw_r, tw_i = times(real_part, imag_part, cosine, sine)
        send_r = jnp.where(upper, tw_r, real_part)
        send_i = jnp.where(upper, tw_i, imag_part)
        other_r, other_i = swapped((send_r, send_i), "ctx", bit)
        real_part = jnp.where(upper, other_r - tw_r, real_part + other_r)
        imag_part = jnp.where(upper, other_i - tw_i, imag_part + other_i)
    return (real_part, imag_part)


def on_device(gate_stream, key_stream, value_stream, residues, decay_rates, out_weight):
    big_p = lax.axis_size("ctx")
    bits = big_p.bit_length() - 1
    rows = key_stream.shape[0]
    length = float(big_p * rows)
    device = lax.axis_index("ctx")
    mixed = jnp.transpose(key_stream.astype(jnp.float32) * value_stream.astype(jnp.float32))
    base, lam, one_less, tail = filter_terms(residues, decay_rates, length)
    filt = (base[:, :, None], lam[:, :, None], one_less[:, :, None], tail[:, :, None])
    z_r, z_i = pre_twiddle(mixed, device, big_p, (2, 1, 1))
    y_r, y_i = butterfly_forward(z_r, z_i, device, bits)
    q_index = reverse_bits(device, bits)
    u_r, u_i = spectral(y_r, y_i, q_index, filt, big_p, rows)
    v_r, v_i = butterfly_inverse(u_r, u_i, device, bits)
    conv_t = post_twiddle(v_r, v_i, device, big_p, rows, (2, 1, 1))
    conv_rows = jnp.transpose(conv_t)
    gated = (gate_stream.astype(jnp.float32) * conv_rows).astype(jnp.bfloat16)
    partial_terms = jnp.dot(gated, out_weight, preferred_element_type=jnp.float32)
    return lax.psum_scatter(partial_terms, "chan", scatter_dimension=1, tiled=True).astype(
        jnp.bfloat16
    )


MESH = pl.DeviceIdType.MESH
LANES = 128
SUB = 8
WIDE = 512
CHUNKS = 16
FORWARDS = 4
SLABS = 4
PIECES = 2


def tree_sum(terms):
    while len(terms) > 1:
        pairs = [terms[i] + terms[i + 1] for i in range(0, len(terms) - 1, 2)]
        terms = pairs + terms[len(pairs) * 2 :]
    return terms[0]


def one_minus_exp(u):
    series = u * (1.0 - u / 2.0 * (1.0 - u / 3.0 * (1.0 - u / 4.0 * (1.0 - u / 5.0 * (1.0 - u / 6.0)))))
    return jnp.where(u > 0.25, 1.0 - jnp.exp(-u), series)


def kernel(
    stages,
    gate_hbm, key_hbm, value_hbm, res_hbm, decay_hbm, w_hbm, out,
    gate, key, value, res, decay, wbuf, sbuf, rbuf, gated,
    xs, ys, lam, base, dec, carried, ends, give, chip, peer_end, zbuf, give_state, peer_state, state,
    in_sem, w_sem, chunk_send, chunk_recv, pair_send, pair_recv, z_send, z_recv,
):
    rows = gate.shape[0]
    modes = res.shape[0]
    half_modes = modes // 2
    half_size = half_modes * SUB
    chan = lax.axis_index("chan")
    ctx = lax.axis_index("ctx")
    core = lax.rem(ctx, 2)
    stage = ctx // 2
    x = lax.rem(chan, 2)
    y = chan // 2
    along_x = y * 2 + (1 - x)
    along_y = (1 - y) * 2 + x
    across = (1 - y) * 2 + (1 - x)
    partner = stage * 2 + (1 - core)

    loads = [
        pltpu.make_async_copy(src, dst, in_sem.at[i])
        for i, (src, dst) in enumerate(
            [(decay_hbm, decay), (res_hbm, res), (gate_hbm, gate)]
        )
    ]
    slab = rows // SLABS

    def stream_load(i):
        src, dst = (key_hbm, key) if i % 2 == 0 else (value_hbm, value)
        here = pl.ds(i // 2 * slab, slab)
        return pltpu.make_async_copy(src.at[here, :], dst.at[here, :], in_sem.at[3 + i])

    for i in range(2 * SLABS):
        stream_load(i).start()
    for load in loads[:2]:
        load.start()

    def w_copy(i):
        owner = (across, along_y if i % 2 else along_x, along_x if i % 2 else along_y, chan)[i // 2]
        column = owner * (2 * WIDE) + (i % 2) * WIDE
        return pltpu.make_async_copy(
            w_hbm.at[:, pl.ds(pl.multiple_of(column, WIDE), WIDE)], wbuf.at[i], w_sem.at[i]
        )

    barrier = pltpu.get_barrier_semaphore()
    pl.semaphore_signal(barrier, inc=1, device_id=(along_x, ctx), device_id_type=MESH)
    pl.semaphore_signal(barrier, inc=1, device_id=(along_y, ctx), device_id_type=MESH)
    pl.semaphore_signal(barrier, inc=1, device_id=(chan, partner), device_id_type=MESH)
    for step in range(1, stages):
        other = lax.rem(stage + step, stages) * 2 + core
        pl.semaphore_signal(barrier, inc=1, device_id=(chan, other), device_id_type=MESH)

    loads[0].wait()
    loads[1].wait()
    for b in range(SUB):
        at = pl.ds(b, modes, stride=SUB)
        d = decay[:, b * LANES : (b + 1) * LANES]
        dec[at, :] = d
        lam[at, :] = jnp.exp(-d)
        base[at, :] = res[:, b * LANES : (b + 1) * LANES] * jnp.sqrt(one_minus_exp(2.0 * d))
    for part in range(SLABS):
        stream_load(2 * part).wait()
        stream_load(2 * part + 1).wait()
        here = slice(part * slab, (part + 1) * slab)
        for b in range(SUB):
            cols = slice(b * LANES, (b + 1) * LANES)
            mixed = key[here, cols].astype(jnp.float32) * value[here, cols].astype(jnp.float32)
            xs[pl.ds(part * slab * SUB + b, slab, stride=SUB), :] = mixed
    loads[2].start()
    for i in range(CHUNKS // 2):
        w_copy(i).start()

    def vec(t):
        return pl.ds(pl.multiple_of(t * SUB, SUB), SUB)

    def mode_rows(half, n):
        return pl.ds(pl.multiple_of(half * half_size + n * SUB, SUB), SUB)

    def half_rows(half):
        return pl.ds(pl.multiple_of(half * half_size, half_size), half_size)

    mid = rows // 2

    quarter = rows // 4
    piece_modes = half_modes // PIECES
    piece_size = piece_modes * SUB

    def end_states(half, piece, dst):
        numbers = range(piece * piece_modes, (piece + 1) * piece_modes)
        lams = [lam[mode_rows(half, n), :] for n in numbers]

        def step(t, carry):
            now = [xs[vec(t + q * quarter), :] for q in range(4)]
            return tuple(tuple(l * h + x for l, h in zip(lams, hidden)) for x, hidden in zip(now, carry))

        zero = tuple(jnp.zeros((SUB, LANES), jnp.float32) for _ in numbers)
        parts = lax.fori_loop(0, quarter, step, (zero,) * 4, unroll=4)
        for k, n in enumerate(numbers):
            shrink = jnp.exp(dec[mode_rows(half, n), :] * float(-quarter))
            total = parts[0][k]
            for q in range(1, 4):
                total = shrink * total + parts[q][k]
            dst[n * SUB : (n + 1) * SUB, :] = total

    def send_end(piece):
        here = pl.ds(piece * piece_size, piece_size)
        return pltpu.make_async_remote_copy(
            src_ref=give.at[here, :], dst_ref=peer_end.at[here, :],
            send_sem=pair_send.at[piece], recv_sem=pair_recv.at[piece],
            device_id=(chan, partner), device_id_type=MESH,
        )

    def push(step, piece):
        here = pl.ds(piece * piece_size, piece_size)
        sem = (step - 1) * PIECES + piece
        return pltpu.make_async_remote_copy(
            src_ref=chip.at[here, :], dst_ref=zbuf.at[step - 1, here, :],
            send_sem=z_send.at[sem], recv_sem=z_recv.at[sem],
            device_id=(chan, lax.rem(stage + step, stages) * 2 + core), device_id_type=MESH,
        )

    is_first = core == 0
    for piece in range(PIECES):
        end_states(1 - core, piece, give)
        if piece == 0:
            pl.semaphore_wait(barrier, 3 + stages - 1)
        send_end(piece).start()

    for piece in range(PIECES):
        end_states(core, piece, ends)
        send_end(piece).wait_recv()
        here = slice(piece * piece_size, (piece + 1) * piece_size)
        rates = dec[pl.ds(pl.multiple_of(core * half_size + piece * piece_size, piece_size), piece_size), :]
        own, peer = ends[here, :], peer_end[here, :]
        chip[here, :] = jnp.exp(rates * float(-rows)) * jnp.where(is_first, own, peer) + jnp.where(is_first, peer, own)
        for step in range(1, stages):
            @pl.when(stage + step < stages)
            def _():
                push(step, piece).start()

    def local_rows(part):
        lams = [lam[n * SUB : (n + 1) * SUB, :] for n in range(modes)]
        bases = [base[n * SUB : (n + 1) * SUB, :] for n in range(modes)]

        def step(t, hidden):
            now = xs[vec(t), :]
            hidden = tuple(l * h + now for l, h in zip(lams, hidden))
            ys[vec(t), :] = tree_sum([b * h for b, h in zip(bases, hidden)])
            return hidden

        if part:
            start = tuple(carried[n * SUB : (n + 1) * SUB, :] for n in range(modes))
        else:
            start = tuple(jnp.zeros((SUB, LANES), jnp.float32) for _ in range(modes))
        hidden = lax.fori_loop(part * mid, (part + 1) * mid, step, start, unroll=4)
        if not part:
            for n in range(modes):
                carried[n * SUB : (n + 1) * SUB, :] = hidden[n]

    local_rows(0)
    state[...] = jnp.zeros_like(state)
    for step in range(1, stages):
        @pl.when(stage >= step)
        def _():
            for piece in range(PIECES):
                push(step, piece).wait_recv()
            weight = jnp.exp(dec[half_rows(core), :] * float(-2 * rows * (step - 1)))
            state[...] += weight * zbuf[step - 1]

    span = jnp.exp(dec[half_rows(core), :] * float(-rows))
    end_first = jnp.where(is_first, ends[...], peer_end[...])
    begin_first = state[...]
    begin_second = span * begin_first + end_first
    give_state[...] = jnp.where(is_first, begin_second, begin_first)
    send_state = pltpu.make_async_remote_copy(
        src_ref=give_state, dst_ref=peer_state, send_sem=pair_send.at[PIECES], recv_sem=pair_recv.at[PIECES],
        device_id=(chan, partner), device_id_type=MESH,
    )
    send_state.start()
    state[...] = jnp.where(is_first, begin_first, begin_second)

    def add_state(half, src, part):
        lams = [lam[mode_rows(half, n), :] for n in range(half_modes)]
        start = part * mid
        low, high = [], []
        for n in range(half_modes):
            d = dec[mode_rows(half, n), :]
            first = base[mode_rows(half, n), :] * src[n * SUB : (n + 1) * SUB, :]
            low.append(first * jnp.exp(d * float(-start)) if part else first)
            high.append(first * jnp.exp(d * float(-start - quarter)))

        def step(t, carry):
            low, high = carry
            low = tuple(l * h for l, h in zip(lams, low))
            high = tuple(l * h for l, h in zip(lams, high))
            ys[vec(t + start), :] += tree_sum(list(low))
            ys[vec(t + start + quarter), :] += tree_sum(list(high))
            return (low, high)

        lax.fori_loop(0, quarter, step, (tuple(low), tuple(high)), unroll=4)

    def gate_rows(part):
        here = slice(part * mid, (part + 1) * mid)
        for b in range(SUB):
            cols = slice(b * LANES, (b + 1) * LANES)
            conv = ys[pl.ds(part * mid * SUB + b, mid, stride=SUB), :]
            gated[here, cols] = (gate[here, cols].astype(jnp.float32) * conv).astype(jnp.bfloat16)

    def chunk_copy(i, target):
        return pltpu.make_async_remote_copy(
            src_ref=sbuf.at[i], dst_ref=rbuf.at[i], send_sem=chunk_send.at[i], recv_sem=chunk_recv.at[i],
            device_id=(target, ctx), device_id_type=MESH,
        )

    def first_target(i):
        odd = lax.rem(i, 2)
        return along_x * (1 - odd) + along_y * odd

    def second_target(i):
        odd = lax.rem(i, 2)
        return along_y * (1 - odd) + along_x * odd

    def w_wait(i):
        pltpu.make_async_copy(w_hbm.at[:, pl.ds(0, WIDE)], wbuf.at[i], w_sem.at[i]).wait()

    def block_of(i):
        return i // 4 * 2 + lax.rem(i, 2)

    def slot_of(i):
        paired = i // 4 * 4 + lax.rem(i, 2) * 2 + lax.rem(i // 2, 2)
        return jnp.where(i // 4 == 1, paired, i)

    def direct_copy(parity):
        both = pl.ds(FORWARDS + 2 * parity, 2)
        return pltpu.make_async_remote_copy(
            src_ref=sbuf.at[both], dst_ref=rbuf.at[both],
            send_sem=chunk_send.at[FORWARDS + parity], recv_sem=chunk_recv.at[FORWARDS + parity],
            device_id=(first_target(parity), ctx), device_id_type=MESH,
        )

    def partial_sum(i):
        part = lax.rem(i // 2, 2)
        here = pl.ds(pl.multiple_of(part * mid, mid), mid)
        sbuf[slot_of(i)] = jnp.dot(gated[here, :], wbuf[block_of(i)], preferred_element_type=jnp.float32)

    add_state(core, state, 0)
    send_state.wait_recv()
    add_state(1 - core, peer_state, 0)
    loads[2].wait()
    gate_rows(0)

    @pl.loop(0, 2)
    def _(i):
        w_wait(i)
        partial_sum(i)
        chunk_copy(i, first_target(i)).start()

    local_rows(1)
    add_state(core, state, 1)
    add_state(1 - core, peer_state, 1)
    gate_rows(1)

    @pl.loop(2, CHUNKS)
    def _(i):
        @pl.when(lax.rem(i // 2, 2) == 0)
        def _():
            w_wait(block_of(i))

        partial_sum(i)

        @pl.when(i < FORWARDS)
        def _():
            chunk_copy(i, first_target(i)).start()

        @pl.when(i // 2 == 3)
        def _():
            direct_copy(lax.rem(i, 2)).start()

    @pl.loop(0, FORWARDS)
    def _(j):
        chunk_copy(j, first_target(j)).wait_recv()
        sbuf[j + 2 * FORWARDS] += rbuf[j]
        chunk_copy(j + 2 * FORWARDS, second_target(j)).start()

    @pl.loop(0, 2)
    def _(parity):
        direct_copy(parity).wait_recv()
        for k in range(2):
            sbuf[3 * FORWARDS + 2 * k + parity] += rbuf[FORWARDS + 2 * parity + k]

    @pl.loop(0, FORWARDS)
    def _(j):
        chunk_copy(j + 2 * FORWARDS, second_target(j)).wait_recv()
        here = pl.ds(pl.multiple_of(j // 2 * mid, mid), mid)
        cols = pl.ds(pl.multiple_of(lax.rem(j, 2) * WIDE, WIDE), WIDE)
        out[here, cols] = (sbuf[j + 3 * FORWARDS] + rbuf[j + 2 * FORWARDS]).astype(jnp.bfloat16)

    for piece in range(PIECES):
        send_end(piece).wait_send()
    send_state.wait_send()
    for parity in range(2):
        direct_copy(parity).wait_send()
    for step in range(1, stages):
        @pl.when(stage + step < stages)
        def _():
            for piece in range(PIECES):
                push(step, piece).wait_send()

    @pl.loop(0, FORWARDS)
    def _(j):
        chunk_copy(j, first_target(j)).wait_send()
        chunk_copy(j + 2 * FORWARDS, second_target(j)).wait_send()


def fused(gate_stream, key_stream, value_stream, residues, decay_rates, out_weight):
    rows, channels = gate_stream.shape
    modes = residues.shape[0]
    stages = lax.axis_size("ctx") // 2
    f32, bf16 = jnp.float32, jnp.bfloat16
    whole = (modes * SUB, LANES)
    half = (modes // 2 * SUB, LANES)
    dma = pltpu.SemaphoreType.DMA
    return pl.pallas_call(
        functools.partial(kernel, stages),
        out_shape=pltpu.VMEM((rows, 2 * WIDE), bf16),
        in_specs=[pl.BlockSpec(memory_space=pltpu.HBM)] * 6,
        out_specs=pl.BlockSpec(memory_space=pltpu.VMEM),
        scratch_shapes=[
            pltpu.VMEM((rows, channels), bf16),
            pltpu.VMEM((rows, channels), bf16),
            pltpu.VMEM((rows, channels), bf16),
            pltpu.VMEM((modes, channels), f32),
            pltpu.VMEM((modes, channels), f32),
            pltpu.VMEM((CHUNKS // 2, channels, WIDE), bf16),
            pltpu.VMEM((CHUNKS, rows // 2, WIDE), f32),
            pltpu.VMEM((3 * FORWARDS, rows // 2, WIDE), f32),
            pltpu.VMEM((rows, channels), bf16),
            pltpu.VMEM((rows * SUB, LANES), f32),
            pltpu.VMEM((rows * SUB, LANES), f32),
            pltpu.VMEM(whole, f32),
            pltpu.VMEM(whole, f32),
            pltpu.VMEM(whole, f32),
            pltpu.VMEM(whole, f32),
            pltpu.VMEM(half, f32),
            pltpu.VMEM(half, f32),
            pltpu.VMEM(half, f32),
            pltpu.VMEM(half, f32),
            pltpu.VMEM((stages - 1,) + half, f32),
            pltpu.VMEM(half, f32),
            pltpu.VMEM(half, f32),
            pltpu.VMEM(half, f32),
            dma((3 + 2 * SLABS,)),
            dma((CHUNKS // 2,)),
            dma((3 * FORWARDS,)),
            dma((3 * FORWARDS,)),
            dma((PIECES + 1,)),
            dma((PIECES + 1,)),
            dma((PIECES * (stages - 1),)),
            dma((PIECES * (stages - 1),)),
        ],
        compiler_params=pltpu.CompilerParams(
            collective_id=0, has_side_effects=True, vmem_limit_bytes=63 * 1024 * 1024
        ),
        cost_estimate=pl.CostEstimate(
            flops=2 * rows * channels * 8 * WIDE, bytes_accessed=2 * channels * 8 * WIDE, transcendentals=0
        ),
    )(gate_stream, key_stream, value_stream, residues, decay_rates, out_weight)


def run(*arrays):
    square = lax.axis_size("chan") == 4 and lax.axis_size("ctx") % 2 == 0 and lax.axis_size("ctx") > 2
    fits = arrays[0].shape[1] == SUB * LANES and arrays[5].shape[1] == 8 * WIDE
    return (fused if square and fits else on_device)(*arrays)


def solution(mesh):
    return jax.shard_map(
        run,
        mesh=mesh,
        in_specs=(
            P("ctx", "chan"),
            P("ctx", "chan"),
            P("ctx", "chan"),
            P(None, "chan"),
            P(None, "chan"),
            P("chan", None),
        ),
        out_specs=P("ctx", "chan"),
        check_vma=False,
    )
```
